32 devices in a mesh: expert: 8 (over z, x), tensor: 4 (over y, core).
Axes of the slice: x: 2, y: 2, z: 4, core: 2. Of those that a mesh axis runs over, the one named last changes fastest.
Arguments:
- tokens: bfloat16 [2048, 4096], P('expert'), may hold values from -6 to 6
- cotangent: bfloat16 [2048, 4096], P('expert'), may hold values from -1.5 to 1.5
- w_in: bfloat16 [4096, 16384], P(None, ('expert', 'tensor')), may hold values from -0.09375 to 0.09375
- w_out: bfloat16 [16384, 4096], P(('expert', 'tensor')), may hold values from -0.09375 to 0.09375
- router: bfloat16 [4096, 4], replicated, may hold values from -0.09375 to 0.09375
- chosen: int32 [4, 512], replicated, may hold values from 0 to 2047, as said below
Outputs:
- grad_tokens: bfloat16 [2048, 4096], P('expert', 'tensor')
- grad_in: bfloat16 [4096, 16384], P(None, ('expert', 'tensor'))
- grad_out: bfloat16 [16384, 4096], P(('expert', 'tensor'))
- grad_router: float32 [4096, 4], replicated
The draws below stay inside these ranges and needn't reach their ends.
Inputs may be any that keep to these rules, and one draw needn't show every extreme that they name: Row e lists, in increasing order, 512 distinct tokens chosen by expert e; at most 128 of them lie among one device's 256 consecutive tokens, and in every row some device's tokens hold exactly 128 of them.
All inputs are finite; a program needn't handle non-finite values.
Results may differ from the reference program's by a relative error of at most 0.005.
Values may be sent and summed in bfloat16 or wider, within the bound.
No kernel may reach another device: no remote copies, remote signals or barrier semaphores. Data moves between devices by JAX's collectives and lax.ppermute only.
A program may use at most 128 MiB of HBM per device.

```python
import jax
import jax.numpy as jnp
from jax import lax

D = 4096
H = 4096
TOK_DEV = 256
EXPERTS = 4
TOKENS = 2048
CAP = 512
MOST = 128


def draw_chosen(key, part):
    home_count = TOKENS // TOK_DEV

    def one_expert(expert_key):
        order_key, forced_key, rank_key = jax.random.split(expert_key, 3)
        forced = jax.random.randint(forced_key, (), 0, home_count)
        order = jax.random.permutation(order_key, home_count * MOST).astype(jnp.int32)
        grid_home = jnp.arange(home_count * MOST, dtype=jnp.int32) // MOST
        order = jnp.where(grid_home == forced, -1 - order, order)
        slot_rank = jnp.argsort(jnp.argsort(order, stable=True), stable=True)
        taken = (slot_rank < CAP).reshape(home_count, MOST)
        counts = jnp.sum(taken.astype(jnp.int32), axis=1)
        ranks = jax.vmap(lambda row_key: jax.random.permutation(row_key, TOK_DEV))(jax.random.split(rank_key, home_count))
        picked = (ranks < counts[:, None]).reshape(-1)
        return jnp.nonzero(picked, size=CAP)[0].astype(jnp.int32)
    return jax.vmap(one_expert)(jax.random.split(key, EXPERTS))


def steps_of(own_key, shape, shards, least, top_value):
    def one(dim, parts):
        steps = jax.random.uniform(jax.random.fold_in(jax.random.fold_in(own_key, 6), dim), (parts,), jnp.float32, least / len(shards), top_value / len(shards))
        return jnp.repeat(jnp.exp(steps), shape[dim] // parts).reshape((-1,) + (1,) * (len(shape) - dim - 1))

    level = one(*shards[0])
    for cut in shards[1:]:
        level = level * one(*cut)
    return level


def scatter_about(stream_key, dims, scale, reach, shards=(), kind=jnp.bfloat16):
    entries = jax.random.normal(stream_key, dims, jnp.float32) * scale
    if len(shards) > 0:
        entries = steps_of(stream_key, dims, shards, -0.22, 0.18) * entries
    return jnp.clip(entries, min=-reach, max=reach).astype(kind)


def setup_inputs(seed: int = 0) -> dict:
    seeds = jax.random.split(jax.random.key(seed), 7)
    return {
        "tokens": scatter_about(seeds[0], (TOKENS, D), 1.0, 6.0, ((0, 8),)),
        "cotangent": scatter_about(seeds[1], (TOKENS, D), 0.25, 1.5, ((0, 8),)),
        "w_in": scatter_about(seeds[2], (D, EXPERTS * H), D ** -0.5, 0.09375, ((1, 32),)),
        "w_out": scatter_about(seeds[3], (EXPERTS * H, D), H ** -0.5, 0.09375, ((0, 32),)),
        "router": scatter_about(seeds[4], (D, EXPERTS), D ** -0.5, 0.09375),
        "chosen": draw_chosen(jax.random.fold_in(seeds[6], 71), 0),
    }


def reference(tokens, cotangent, w_in, w_out, router, chosen):
    def per_expert(total, expert):
        rows = chosen[expert]
        x_rows = tokens[rows]
        y_rows = cotangent[rows]
        w_first = lax.dynamic_slice_in_dim(w_in, expert * H, H, 1)
        w_second = lax.dynamic_slice_in_dim(w_out, expert * H, H, 0)
        r_col = lax.dynamic_slice_in_dim(router, expert, 1, 1)
        gate = jax.nn.sigmoid(jnp.dot(x_rows, r_col, preferred_element_type=jnp.float32)[:, 0])
        pre_act = jnp.dot(x_rows, w_first, preferred_element_type=jnp.float32)
        sig_act = jax.nn.sigmoid(pre_act)
        hidden = pre_act * sig_act
        upstream = jnp.dot(y_rows, w_second.T, preferred_element_type=jnp.float32)
        gated_hidden = (gate[:, None] * hidden).astype(jnp.bfloat16)
        gate_grad = jnp.sum(hidden * upstream, axis=1)
        pre_grad = (gate[:, None] * upstream * sig_act * (1.0 + pre_act * (1.0 - sig_act))).astype(jnp.bfloat16)
        grad_second = jnp.dot(gated_hidden.T, y_rows, preferred_element_type=jnp.float32).astype(jnp.bfloat16)
        grad_first = jnp.dot(x_rows.T, pre_grad, preferred_element_type=jnp.float32).astype(jnp.bfloat16)
        score_grad = gate_grad * gate * (1.0 - gate)
        router_col = jnp.dot(score_grad, x_rows.astype(jnp.float32), precision=lax.Precision.HIGHEST)
        row_grad = jnp.dot(pre_grad, w_first.T, preferred_element_type=jnp.float32)
        row_grad = row_grad + score_grad[:, None] * r_col[:, 0].astype(jnp.float32)[None, :]
        total = total.at[rows].add(row_grad)
        return total, (grad_first, grad_second, router_col)

    start = jnp.zeros((TOKENS, D), jnp.float32)
    total, (grad_first, grad_second, router_cols) = lax.scan(per_expert, start, jnp.arange(EXPERTS, dtype=jnp.int32))
    grad_tokens = total.astype(jnp.bfloat16)
    grad_in = jnp.transpose(grad_first, (1, 0, 2)).reshape(D, EXPERTS * H)
    grad_out = grad_second.reshape(EXPERTS * H, D)
    grad_router = router_cols.T
    return (grad_tokens, grad_in, grad_out, grad_router)
```

```python
import functools

import jax
import jax.numpy as jnp
from jax import lax
from jax.experimental import pallas as pl
from jax.experimental.pallas import tpu as pltpu
from jax.sharding import Mesh
from jax.sharding import PartitionSpec as P

BF = jnp.bfloat16
F32 = jnp.float32
CORE = 2
VMEM_LIMIT = 40 * 1024 * 1024


def params():
    return pltpu.CompilerParams(vmem_limit_bytes=VMEM_LIMIT)


def full(shape):
    return pl.BlockSpec(shape, lambda *_: (0,) * len(shape))


def cost(flops, moved):
    return pl.CostEstimate(flops=int(flops), bytes_accessed=int(moved), transcendentals=0)


def dot(a, b, da, db):
    return lax.dot_general(a, b, (((da,), (db,)), ((), ())), preferred_element_type=F32)


def flip(x, bit):
    if bit == 1:
        return lax.ppermute(x, "half", [(0, 1), (1, 0)])
    n = lax.axis_size("tensor")
    return lax.ppermute(x, "tensor", [(i, i ^ (bit >> 1)) for i in range(n)])


def shift(x, step):
    n = lax.axis_size("plane")
    return lax.ppermute(x, "plane", [(i, (i + step) % n) for i in range(n)])


def chip_masks(slots):
    return sorted((m for m in range(slots) if not m & CORE), key=lambda m: (m.bit_count(), m))


def top_bit(m):
    return 1 << (m.bit_length() - 1)


def plane_gather(own, slots):
    half = own.shape[0] // 2
    blocks = {0: own}
    for m in chip_masks(slots)[1:]:
        low, high = m & -m, top_bit(m)
        if low == high:
            blocks[m] = flip(own, m)
        else:
            blocks[m] = jnp.concatenate(
                [flip(blocks[m ^ low][:half], low), flip(blocks[m ^ high][half:], high)]
            )
    for m in chip_masks(slots):
        blocks[m | CORE] = flip(blocks[m], CORE)
    return blocks


def ring_gather(x, n):
    rows = x.shape[0]
    half = rows // 2
    pieces = [(0, 0, x)]
    up, down = x, x
    for k in range(1, (n + 1) // 2):
        up, down = shift(up, 1), shift(down, -1)
        pieces += [(k, 0, up), (n - k, 0, down)]
    pieces += [(n // 2, 0, shift(up[:half], 1)), (n // 2, half, shift(down[half:], -1))]
    return pieces


def compact(chosen_col, starts, pieces):
    cap = chosen_col.shape[0]
    width = pieces[0].shape[1]

    def kernel(starts_ref, chosen_ref, *refs):
        out = refs[-1]
        acc = None
        for i, piece in enumerate(refs[:-1]):
            rows = piece.shape[0]
            place = chosen_ref[...] - starts_ref[i]
            hot = lax.broadcasted_iota(jnp.int32, (cap, rows), 1) == place
            term = dot(hot.astype(F32).astype(BF), piece[...], 1, 0)
            acc = term if acc is None else acc + term
        out[...] = acc.astype(BF)

    total = sum(p.shape[0] for p in pieces)
    return pl.pallas_call(
        kernel,
        grid_spec=pltpu.PrefetchScalarGridSpec(
            num_scalar_prefetch=1,
            grid=(1,),
            in_specs=[full(chosen_col.shape)] + [full(p.shape) for p in pieces],
            out_specs=full((cap, width)),
        ),
        out_shape=jax.ShapeDtypeStruct((cap, width), BF),
        compiler_params=params(),
        cost_estimate=cost(2 * cap * total * width, 2 * (cap + total) * width),
        name="compact_rows",
    )(starts, chosen_col, *pieces)


def place(chosen_row, starts, sizes, terms):
    cap, width = terms[0].shape

    def kernel(starts_ref, chosen_ref, *refs):
        ins, outs = refs[: len(terms)], refs[len(terms) :]
        total = ins[0][...].astype(F32)
        for r in ins[1:]:
            total = total + r[...].astype(F32)
        rows = total.astype(BF)
        for i, out in enumerate(outs):
            n = out.shape[0]
            spot = chosen_ref[...] - starts_ref[i]
            hot = lax.broadcasted_iota(jnp.int32, (n, cap), 0) == spot
            out[...] = dot(hot.astype(F32).astype(BF), rows, 1, 0).astype(BF)

    total = sum(sizes)
    return pl.pallas_call(
        kernel,
        grid_spec=pltpu.PrefetchScalarGridSpec(
            num_scalar_prefetch=1,
            grid=(1,),
            in_specs=[full(chosen_row.shape)] + [full(t.shape) for t in terms],
            out_specs=[full((n, width)) for n in sizes],
        ),
        out_shape=[jax.ShapeDtypeStruct((n, width), BF) for n in sizes],
        compiler_params=params(),
        cost_estimate=cost(2 * cap * total * width, 2 * (cap + total) * width),
        name="place_rows",
    )(starts, chosen_row, *terms)


def project_in(order, expert, xs, w_in, router):
    cap, width = xs[0].shape
    hidden = w_in.shape[1]
    experts = router.shape[1]
    count = len(xs)

    def kernel(order_ref, expert_ref, *refs):
        ins = refs[:count]
        w_ref, r_ref, a_ref, gate_ref, score = refs[count:]
        j = pl.program_id(0)

        @pl.when(j == 0)
        def _():
            a_ref[...] = jnp.zeros_like(a_ref)
            score[...] = jnp.zeros_like(score)

        for k in range(count):

            @pl.when(j == k)
            def _():
                a_ref[...] += dot(ins[k][...], w_ref[...], 1, 0)
                score[...] += dot(ins[k][...], r_ref[...], 1, 0)

        @pl.when(j == count - 1)
        def _():
            mine = lax.broadcasted_iota(jnp.int32, (cap, experts), 1) == expert_ref[0]
            picked = jnp.sum(jnp.where(mine, score[...], 0.0), axis=1, keepdims=True)
            gate_ref[...] = jax.nn.sigmoid(picked)

    return pl.pallas_call(
        kernel,
        grid_spec=pltpu.PrefetchScalarGridSpec(
            num_scalar_prefetch=2,
            grid=(count,),
            in_specs=[full((cap, width))] * count
            + [
                pl.BlockSpec((width, hidden), lambda j, order, _: (order[j], 0)),
                pl.BlockSpec((width, experts), lambda j, order, _: (order[j], 0)),
            ],
            out_specs=[full((cap, hidden)), full((cap, 1))],
            scratch_shapes=[pltpu.VMEM((cap, experts), F32)],
        ),
        out_shape=[jax.ShapeDtypeStruct((cap, hidden), F32), jax.ShapeDtypeStruct((cap, 1), F32)],
        compiler_params=params(),
        cost_estimate=cost(2 * cap * width * count * hidden, 2 * width * count * (cap + hidden)),
        name="project_in",
    )(order, expert, *xs, w_in, router)


def project_out(order, ys, w_out, pre_act, gate):
    cap, width = ys[0].shape
    hidden = w_out.shape[0]
    count = len(ys)

    def kernel(order_ref, *refs):
        ins = refs[:count]
        w_ref, a_ref, gate_ref, hg_ref, da_ref, ds_ref, up = refs[count:]
        j = pl.program_id(0)

        @pl.when(j == 0)
        def _():
            up[...] = jnp.zeros_like(up)

        for k in range(count):

            @pl.when(j == k)
            def _():
                up[...] += dot(ins[k][...], w_ref[...], 1, 1)

        @pl.when(j == count - 1)
        def _():
            a = a_ref[...]
            u = up[...]
            gate = gate_ref[...]
            sig = jax.nn.sigmoid(a)
            act = a * sig
            hg_ref[...] = (gate * act).astype(BF)
            gate_grad = jnp.sum(act * u, axis=1, keepdims=True)
            ds_ref[...] = gate_grad * gate * (1.0 - gate)
            da_ref[...] = (gate * u * sig * (1.0 + a * (1.0 - sig))).astype(BF)

    return pl.pallas_call(
        kernel,
        grid_spec=pltpu.PrefetchScalarGridSpec(
            num_scalar_prefetch=1,
            grid=(count,),
            in_specs=[full((cap, width))] * count
            + [
                pl.BlockSpec((hidden, width), lambda j, order: (0, order[j])),
                full((cap, hidden)),
                full((cap, 1)),
            ],
            out_specs=[full((cap, hidden)), full((cap, hidden)), full((cap, 1))],
            scratch_shapes=[pltpu.VMEM((cap, hidden), F32)],
        ),
        out_shape=[
            jax.ShapeDtypeStruct((cap, hidden), BF),
            jax.ShapeDtypeStruct((cap, hidden), BF),
            jax.ShapeDtypeStruct((cap, 1), F32),
        ],
        compiler_params=params(),
        cost_estimate=cost(2 * cap * width * count * hidden, 2 * width * count * (cap + hidden)),
        name="project_out",
    )(order, *ys, w_out, pre_act, gate)


def row_grads(order, pre_grad, score_grad, w_in, router_row, arrived, kinds):
    cap, hidden = pre_grad.shape
    count = len(kinds)
    width = w_in.shape[0] // (2 * lax.axis_size("tensor"))
    extra = [] if arrived is None else [arrived]

    def kernel(order_ref, da_ref, ds_ref, w_ref, r_ref, *refs):
        outs = refs[len(extra) :]
        j = pl.program_id(0)
        block = dot(da_ref[...], w_ref[...], 1, 1) + ds_ref[...] * r_ref[...]
        if extra:
            block = block + refs[0][0].astype(F32)
        for k in range(count):

            @pl.when(j == k)
            def _():
                outs[k][...] = block.astype(kinds[k])

    return pl.pallas_call(
        kernel,
        grid_spec=pltpu.PrefetchScalarGridSpec(
            num_scalar_prefetch=1,
            grid=(count,),
            in_specs=[
                full((cap, hidden)),
                full((cap, 1)),
                pl.BlockSpec((width, hidden), lambda j, order: (order[j], 0)),
                pl.BlockSpec((1, width), lambda j, order: (0, order[j])),
            ]
            + [pl.BlockSpec((1, cap, width), lambda j, order: (j, 0, 0)) for _ in extra],
            out_specs=[full((cap, width)) for _ in kinds],
        ),
        out_shape=[jax.ShapeDtypeStruct((cap, width), kind) for kind in kinds],
        compiler_params=params(),
        cost_estimate=cost(2 * cap * width * count * hidden, 4 * width * count * (cap + hidden)),
        name="row_grads",
    )(order, pre_grad, score_grad, w_in, router_row, *extra)


def grads_in(order, xs, pre_grad, score_grad):
    cap, width = xs[0].shape
    hidden = pre_grad.shape[1]
    count = len(xs)

    def kernel(order_ref, *refs):
        ins = refs[:count]
        da_ref, ds_ref, out, col = refs[count:]
        j = pl.program_id(0)
        for k in range(count):

            @pl.when(j == k)
            def _():
                x = ins[k][...]
                out[...] = dot(x, da_ref[...], 0, 0).astype(BF)
                col[...] = jnp.sum(x.astype(F32) * ds_ref[...], axis=0, keepdims=True)

    return pl.pallas_call(
        kernel,
        grid_spec=pltpu.PrefetchScalarGridSpec(
            num_scalar_prefetch=1,
            grid=(count,),
            in_specs=[full((cap, width))] * count + [full((cap, hidden)), full((cap, 1))],
            out_specs=[
                pl.BlockSpec((width, hidden), lambda j, order: (order[j], 0)),
                pl.BlockSpec((1, width), lambda j, order: (0, order[j])),
            ],
        ),
        out_shape=[
            jax.ShapeDtypeStruct((width * count, hidden), BF),
            jax.ShapeDtypeStruct((1, width * count), F32),
        ],
        compiler_params=params(),
        cost_estimate=cost(2 * cap * width * count * hidden, 2 * width * count * (cap + hidden)),
        name="grads_in",
    )(order, *xs, pre_grad, score_grad)


def grads_out(order, ys, gated):
    cap, width = ys[0].shape
    hidden = gated.shape[1]
    count = len(ys)

    def kernel(order_ref, *refs):
        ins = refs[:count]
        hg_ref, out = refs[count:]
        j = pl.program_id(0)
        for k in range(count):

            @pl.when(j == k)
            def _():
                out[...] = dot(hg_ref[...], ins[k][...], 0, 0).astype(BF)

    return pl.pallas_call(
        kernel,
        grid_spec=pltpu.PrefetchScalarGridSpec(
            num_scalar_prefetch=1,
            grid=(count,),
            in_specs=[full((cap, width))] * count + [full((cap, hidden))],
            out_specs=pl.BlockSpec((hidden, width), lambda j, order: (0, order[j])),
        ),
        out_shape=jax.ShapeDtypeStruct((hidden, width * count), BF),
        compiler_params=params(),
        cost_estimate=cost(2 * cap * width * count * hidden, 2 * width * count * (cap + hidden)),
        name="grads_out",
    )(order, *ys, gated)


def body(tokens, cotangent, w_in, w_out, router, chosen):
    planes = lax.axis_size("plane")
    slots = 2 * lax.axis_size("tensor")
    tok_dev, features = tokens.shape
    width = features // slots
    cap = chosen.shape[1]
    plane = lax.axis_index("plane")
    half = lax.axis_index("half")
    slot = lax.axis_index("tensor") * 2 + half
    expert = plane.astype(jnp.int32)[None]
    chosen_col = lax.dynamic_slice_in_dim(chosen.T, plane, 1, 1)
    chosen_row = lax.dynamic_slice_in_dim(chosen, plane, 1, 0)
    router_row = lax.dynamic_slice_in_dim(router.T, plane, 1, 0).astype(F32)
    masks = chip_masks(slots)

    def fetch(source):
        own = lax.dynamic_slice_in_dim(source, slot * width, width, 1)
        away = flip(lax.dynamic_slice_in_dim(source, (slot ^ 1) * width, width, 1), 1)
        pieces = [(0, p) for p in ring_gather(own, planes)] + [(1, p) for p in ring_gather(away, planes)]
        starts = jnp.stack(
            [
                (((plane - back) % planes) * 2 + (half ^ other)) * tok_dev + offset
                for other, (back, offset, _) in pieces
            ]
        ).astype(jnp.int32)
        return plane_gather(compact(chosen_col, starts, [x for _, (_, _, x) in pieces]), slots)

    xs = fetch(tokens)
    ys = fetch(cotangent)
    keys = masks + [m | CORE for m in masks]
    order = jnp.stack([slot ^ m for m in keys]).astype(jnp.int32)
    x_list = [xs[m] for m in keys]
    y_list = [ys[m] for m in keys]
    pre_act, gate = project_in(order, expert, x_list, w_in, router)
    gated, pre_grad, score_grad = project_out(order, y_list, w_out, pre_act, gate)

    back = masks[::-1]
    far = jnp.stack([slot ^ m ^ CORE for m in back]).astype(jnp.int32)
    near = jnp.stack([slot ^ m for m in back]).astype(jnp.int32)
    sent = row_grads(far, pre_grad, score_grad, w_in, router_row, None, [BF] * len(back))
    arrived = flip(jnp.stack(sent), CORE)
    kinds = [BF if i == 0 else F32 for i in range(len(back))]
    sums = dict(zip(back, row_grads(near, pre_grad, score_grad, w_in, router_row, arrived, kinds)))
    mid = cap // 2
    last = [sums[0]]
    for m in back[:-1]:
        low, high = m & -m, top_bit(m)
        block = sums[m].astype(BF)
        if low == high:
            last.append(flip(block, m))
            continue
        a, b = flip(block[:mid], low), flip(block[mid:], high)
        for key, piece, first in ((m ^ low, a, True), (m ^ high, b, False)):
            old = sums[key].astype(F32)
            parts = [old[:mid], old[mid:]]
            parts[0 if first else 1] = parts[0 if first else 1] + piece.astype(F32)
            sums[key] = jnp.concatenate(parts)

    shape = [(1, n, o, r) for n, o, r in ring_shape(planes, tok_dev)]
    shape += [(0, n, o, r) for n, o, r in ring_shape(planes, tok_dev)]
    starts = jnp.stack(
        [(((plane + n) % planes) * 2 + (half ^ other)) * tok_dev + o for other, n, o, _ in shape]
    ).astype(jnp.int32)
    placed = place(chosen_row, starts, [r for *_, r in shape], last)
    count = len(shape) // 2
    away = ring_scatter(placed[:count], planes)
    away = flip(away, 1)
    own = ring_scatter(placed[count:], planes)
    grad_tokens = jnp.where(
        half == 0, jnp.concatenate([own, away], axis=1), jnp.concatenate([away, own], axis=1)
    )

    grad_in, router_col = grads_in(order, x_list, pre_grad, score_grad)
    grad_out = grads_out(order, y_list, gated)
    total = jnp.where(jnp.arange(planes)[:, None] == plane, router_col, 0.0)
    bit = 1
    while bit < slots:
        total = total + flip(total, bit)
        bit *= 2
    bit = 1
    while bit < planes:
        total = total + lax.ppermute(total, "plane", [(i, i ^ bit) for i in range(planes)])
        bit *= 2
    return (grad_tokens, grad_in, grad_out, total.T)


def ring_shape(n, rows):
    half = rows // 2
    return [(0, 0, rows), (n // 2, 0, half), (n // 2, half, half)] + [
        piece for k in range(n // 2 - 1, 0, -1) for piece in ((k, 0, rows), (n - k, 0, rows))
    ]


def ring_scatter(pieces, n):
    own, up, down = pieces[:3]
    half = own.shape[0] // 2
    up, down = shift(up, 1).astype(F32), shift(down, -1).astype(F32)
    rest = pieces[3:]
    for k in range(0, len(rest), 2):
        ahead, behind = rest[k].astype(F32), rest[k + 1].astype(F32)
        if up.shape[0] == half:
            ahead = jnp.concatenate([ahead[:half] + up, ahead[half:]])
            behind = jnp.concatenate([behind[:half], behind[half:] + down])
        else:
            ahead, behind = ahead + up, behind + down
        up, down = shift(ahead.astype(BF), 1).astype(F32), shift(behind.astype(BF), -1).astype(F32)
    own = own.astype(F32)
    if up.shape[0] == half:
        return (own + jnp.concatenate([up, down])).astype(BF)
    return (own + up + down).astype(BF)


def solution(mesh):
    planes = mesh.shape["expert"] // 2
    inner = Mesh(mesh.devices.reshape(planes, 2, mesh.shape["tensor"]), ("plane", "half", "tensor"))
    home = ("plane", "half")
    every = ("plane", "half", "tensor")
    return jax.shard_map(
        body,
        mesh=inner,
        in_specs=(P(home, None), P(home, None), P(None, every), P(every, None), P(), P()),
        out_specs=(P(home, "tensor"), P(None, every), P(every, None), P()),
        check_vma=False,
    )
```

```python
import functools
import math

import jax
import jax.numpy as jnp
from jax import lax
from jax.experimental import pallas as pl
from jax.experimental.pallas import tpu as pltpu
from jax.sharding import Mesh
from jax.sharding import PartitionSpec as P

BF = jnp.bfloat16
F32 = jnp.float32
CORE = 2
VMEM_LIMIT = 24 * 1024 * 1024


def dot(a, b, da, db):
    return lax.dot_general(a, b, (((da,), (db,)), ((), ())), preferred_element_type=F32)


def flip(x, bit):
    if bit == 1:
        return lax.ppermute(x, "half", [(0, 1), (1, 0)])
    n = lax.axis_size("tensor")
    return lax.ppermute(x, "tensor", [(i, i ^ (bit >> 1)) for i in range(n)])


def chip_masks(slots):
    return sorted((m for m in range(slots) if not m & CORE), key=lambda m: (m.bit_count(), m))


def top_bit(m):
    return 1 << (m.bit_length() - 1)


def plane_gather(own, slots, *before):
    half = own.shape[0] // 2
    blocks = {0: [(0, own)]}
    for m in chip_masks(slots)[1:]:
        low, high = m & -m, top_bit(m)
        if low == high:
            blocks[m] = [(0, flip(own, m))]
        else:
            first = rows_of(blocks[m ^ low], 0, half)
            second = rows_of(blocks[m ^ high], half, half)
            if before:
                first, second = after(first, *before), after(second, *before)
            blocks[m] = [(0, flip(first, low)), (half, flip(second, high))]
    for m in chip_masks(slots):
        blocks[m | CORE] = [(at, flip(x, CORE)) for at, x in blocks[m]]
    return blocks


def rows_of(pieces, start, count):
    for at, x in pieces:
        if at == start and x.shape[0] == count:
            return x
        if at <= start and start + count <= at + x.shape[0]:
            return x[start - at : start - at + count]
    raise ValueError("rows split")


def after(x, *others):
    return lax.optimization_barrier((x, *others))[0]


def join(*arrays):
    return lax.optimization_barrier(arrays)


class Tiles:
    def __init__(self, x, axis, count, first=0):
        self.x, self.axis, self.count, self.first = x, axis, count, first
        self.size = x.shape[axis] // (2 * lax.axis_size("tensor"))

    def at(self, ref, order_ref, j):
        here = block_at(order_ref[self.first + j], self.size)
        return ref.at[here, :] if self.axis == 0 else ref.at[:, here]


def call(kernel, name, flops, outs, smem, *args):
    flat_args = list(smem)
    for x in args:
        if isinstance(x, Tiles):
            x = x.x
        elif isinstance(x, list):
            x = pltpu.with_memory_space_constraint(x[0], pltpu.HBM)
        flat_args.append(x)

    def run(*refs):
        scalars, refs = refs[: len(smem)], list(refs[len(smem) :])
        for i, x in enumerate(args):
            if isinstance(x, Tiles):
                refs[i] = [x.at(refs[i], scalars[0], j) for j in range(x.count)]
        kernel(*scalars, *refs)

    moved = sum(a.size * a.dtype.itemsize for a in flat_args) + 4 * sum(math.prod(o.shape) for o in outs)
    return pl.pallas_call(
        run,
        in_specs=[pl.BlockSpec(memory_space=pltpu.SMEM)] * len(smem)
        + [pl.BlockSpec(memory_space=pltpu.VMEM)] * len(args),
        out_specs=[pl.BlockSpec(memory_space=pltpu.VMEM)] * len(outs),
        out_shape=outs,
        compiler_params=pltpu.CompilerParams(vmem_limit_bytes=VMEM_LIMIT),
        cost_estimate=pl.CostEstimate(flops=int(flops), bytes_accessed=int(moved), transcendentals=0),
        name=name,
    )(*flat_args)


def shaped(*shape, dtype=F32):
    return jax.ShapeDtypeStruct(shape, dtype)


def block_at(start, size):
    return pl.ds(pl.multiple_of(start * size, size), size)


def stage(*arrays):
    def kernel(*refs):
        sources, results, ready = refs[: len(arrays)], refs[len(arrays) : -1], refs[-1]
        copies = [
            pltpu.make_async_copy(x, y, ready.at[i]) for i, (x, y) in enumerate(zip(sources, results))
        ]
        for copy in copies:
            copy.start()
        for copy in copies:
            copy.wait()

    return pl.pallas_call(
        kernel,
        in_specs=[pl.BlockSpec(memory_space=pltpu.HBM)] * len(arrays),
        out_specs=[pl.BlockSpec(memory_space=pltpu.VMEM)] * len(arrays),
        out_shape=[pltpu.VMEM(x.shape, x.dtype) for x in arrays],
        scratch_shapes=[pltpu.SemaphoreType.DMA((len(arrays),))],
        compiler_params=pltpu.CompilerParams(vmem_limit_bytes=VMEM_LIMIT),
        cost_estimate=pl.CostEstimate(
            flops=0, bytes_accessed=sum(2 * x.size * x.dtype.itemsize for x in arrays), transcendentals=0
        ),
        name="stage_weights",
    )(*arrays)


def pack(firsts, chosen_cols, source, bucket):
    experts = chosen_cols.shape[1]
    rows, features = source.shape
    width = features // 2

    def kernel(firsts_ref, chosen_ref, source_ref, out, hot_out):
        for e in range(experts):
            picked = chosen_ref[pl.ds(firsts_ref[e + 1], bucket), :][:, e : e + 1] - firsts_ref[0]
            hot = lax.broadcasted_iota(jnp.int32, (bucket, rows), 1) == picked
            hot = hot.astype(F32).astype(BF)
            hot_out[e] = hot
            got = dot(hot, source_ref[...], 1, 0).astype(BF)
            out[2 * e], out[2 * e + 1] = got[:, :width], got[:, width:]

    flops = 2 * experts * bucket * rows * features
    outs = [
        shaped(2 * experts, bucket, width, dtype=BF),
        shaped(experts, bucket, rows, dtype=BF),
    ]
    return call(kernel, "pack_rows", flops, outs, [firsts], chosen_cols, source)


def compact(reach, buckets, cap):
    homes, bucket, width = buckets.shape

    def kernel(reach_ref, buckets_ref, out):
        acc = None
        for s in range(homes):
            at = lax.broadcasted_iota(jnp.int32, (cap, bucket), 0) - reach_ref[s]
            hot = lax.broadcasted_iota(jnp.int32, (cap, bucket), 1) == at
            term = dot(hot.astype(F32).astype(BF), buckets_ref[s], 1, 0)
            acc = term if acc is None else acc + term
        out[...] = acc.astype(BF)

    flops = 2 * cap * homes * bucket * width
    outs = [shaped(cap, width, dtype=BF)]
    return call(kernel, "compact_rows", flops, outs, [reach], buckets)[0]


def place(reach, homes, bucket, terms):
    cap, width = terms[0].shape

    def kernel(reach_ref, *refs):
        total = refs[0][...].astype(F32)
        for r in refs[1:-1]:
            total = total + r[...].astype(F32)
        rows = total.astype(BF)
        for s in range(homes):
            at = lax.broadcasted_iota(jnp.int32, (bucket, cap), 1) - reach_ref[s]
            hot = lax.broadcasted_iota(jnp.int32, (bucket, cap), 0) == at
            refs[-1][s] = dot(hot.astype(F32).astype(BF), rows, 1, 0).astype(BF)

    flops = 2 * cap * homes * bucket * width
    outs = [shaped(homes, bucket, width, dtype=BF)]
    return call(kernel, "place_rows", flops, outs, [reach], *terms)[0]


def combine(hots, returned):
    experts, bucket, rows = hots.shape
    width = returned.shape[2]

    def kernel(hots_ref, returned_ref, out):
        for h in range(2):
            acc = None
            for e in range(experts):
                term = dot(hots_ref[e], returned_ref[2 * e + h], 0, 0)
                acc = term if acc is None else acc + term
            out[:, h * width : (h + 1) * width] = acc.astype(BF)

    flops = 4 * experts * bucket * rows * width
    outs = [shaped(rows, 2 * width, dtype=BF)]
    return call(kernel, "combine_rows", flops, outs, [], hots, returned)[0]


def flat(blocks, keys):
    spots = [(j, at, x.shape[0]) for j, m in enumerate(keys) for at, x in blocks[m]]
    return spots, [x for m in keys for _, x in blocks[m]]


def add_rows(total, at, rows, values):
    done = []
    for start, old in total:
        size = old.shape[0]
        if at <= start and start + size <= at + rows:
            done.append((start, old + values[start - at : start - at + size]))
        elif start <= at and at + rows <= start + size:
            cuts = [(start, old[: at - start]), (at, old[at - start : at - start + rows] + values)]
            cuts.append((at + rows, old[at - start + rows :]))
            done += [c for c in cuts if c[1].shape[0]]
        else:
            done.append((start, old))
    return done


def product(spots, ins, tiles, side):
    total = None
    for (j, at, rows), x in zip(spots, ins):
        term = dot(x[...], tiles[j][...], 1, side)
        total = [(at, term)] if total is None else add_rows(total, at, rows, term)
    return total


def project_in(order, expert, blocks, keys, w_in, router):
    spots, xs = flat(blocks, keys)
    cap, width = blocks[0][0][1].shape
    hidden = w_in.shape[1]
    experts = router.shape[1]

    def kernel(order_ref, expert_ref, *refs):
        ins, (tiles, r_ref, a_ref, gate_ref) = refs[: len(xs)], refs[len(xs) :]
        scores = None
        for (j, at, rows), x in zip(spots, ins):
            s = dot(x[...], r_ref[block_at(order_ref[j], width), :], 1, 0)
            scores = [(at, s)] if scores is None else add_rows(scores, at, rows, s)
            a = dot(x[...], tiles[j][...], 1, 0)
            if j == 0:
                a_ref[at : at + rows, :] = a
            else:
                a_ref[at : at + rows, :] += a
        for at, s in scores:
            mine = lax.broadcasted_iota(jnp.int32, s.shape, 1) == expert_ref[0]
            picked = jnp.sum(jnp.where(mine, s, 0.0), axis=1, keepdims=True)
            gate_ref[at : at + s.shape[0], :] = jax.nn.sigmoid(picked)

    flops = 2 * cap * width * len(keys) * hidden
    outs = [shaped(cap, hidden), shaped(cap, 1)]
    tiles = Tiles(w_in, 0, len(keys))
    return call(kernel, "project_in", flops, outs, [order, expert], *[[x] for x in xs], tiles, router)


def project_out(order, blocks, keys, w_out):
    spots, ys = flat(blocks, keys)
    cap, width = blocks[0][0][1].shape
    hidden = w_out.shape[0]

    def kernel(order_ref, *refs):
        ins, (tiles, up) = refs[: len(ys)], refs[len(ys) :]
        for (j, at, rows), y in zip(spots, ins):
            u = dot(y[...], tiles[j][...], 1, 1)
            if j == 0:
                up[at : at + rows, :] = u
            else:
                up[at : at + rows, :] += u

    flops = 2 * cap * width * len(keys) * hidden
    tiles = Tiles(w_out, 1, len(keys))
    return call(kernel, "project_out", flops, [shaped(cap, hidden)], [order], *ys, tiles)[0]


def activation(order, blocks, keys, far, near, w_out, w_in, router_row, upstream, pre_act, gate):
    spots, ys = flat(blocks, keys)
    width = blocks[0][0][1].shape[1]
    cap, hidden = pre_act.shape
    count = sum(far) + sum(near)

    def kernel(order_ref, *refs):
        ins, refs = refs[: len(ys)], refs[len(ys) :]
        tiles, back, r_ref, u_ref, a_ref, gate_ref, hg_ref, da_ref, ds_ref, *outs = refs
        up = [(0, u_ref[...])]
        for (j, at, rows), y in zip(spots, ins):
            up = add_rows(up, at, rows, dot(y[...], tiles[j][...], 1, 1))
        for at, u in up:
            place = slice(at, at + u.shape[0])
            a = a_ref[place, :]
            gate = gate_ref[place, :]
            sig = jax.nn.sigmoid(a)
            act = a * sig
            hg_ref[place, :] = (gate * act).astype(BF)
            gate_grad = jnp.sum(act * u, axis=1, keepdims=True)
            ds_ref[place, :] = gate_grad * gate * (1.0 - gate)
            da_ref[place, :] = (gate * u * sig * (1.0 + a * (1.0 - sig))).astype(BF)
        places = [(out, k) for out, n in zip(outs, far + near) for k in range(n)]
        for k, (out, spot) in enumerate(places):
            here = block_at(order_ref[len(keys) + k], width)
            block = dot(da_ref[...], back[k][...], 1, 1) + ds_ref[...] * r_ref[:, here]
            out[spot] = block.astype(out.dtype)

    flops = 2 * cap * width * (len(keys) + count) * hidden
    outs = [shaped(cap, hidden, dtype=BF), shaped(cap, hidden, dtype=BF), shaped(cap, 1)]
    outs += [shaped(n, cap, width, dtype=BF) for n in far] + [shaped(n, cap, width) for n in near]
    tiles, back = Tiles(w_out, 1, len(keys)), Tiles(w_in, 0, count, len(keys))
    more = (tiles, back, router_row, upstream, pre_act, gate)
    return call(kernel, "activation", flops, outs, [order], *ys, *more)


def router_column(order, blocks, keys, score_grad):
    spots, xs = flat(blocks, keys)
    width = blocks[0][0][1].shape[1]

    def kernel(order_ref, *refs):
        ins, (ds_ref, col) = refs[: len(xs)], refs[len(xs) :]
        for j in range(len(keys)):
            line = None
            for (k, at, rows), x in zip(spots, ins):
                if k == j:
                    c = jnp.sum(x[...].astype(F32) * ds_ref[at : at + rows, :], axis=0, keepdims=True)
                    line = c if line is None else line + c
            col[:, block_at(order_ref[j], width)] = line

    flops = 2 * score_grad.shape[0] * width * len(keys)
    outs = [shaped(1, width * len(keys))]
    return call(kernel, "router_column", flops, outs, [order], *[[x] for x in xs], score_grad)[0]


def grads_in(order, blocks, keys, pre_grad):
    spots, xs = flat(blocks, keys)
    cap, width = blocks[0][0][1].shape
    hidden = pre_grad.shape[1]

    def kernel(order_ref, *refs):
        ins, (da_ref, out) = refs[: len(xs)], refs[len(xs) :]
        for j in range(len(keys)):
            grad = None
            for (k, at, rows), x in zip(spots, ins):
                if k == j:
                    g = dot(x[...], da_ref[at : at + rows, :], 0, 0)
                    grad = g if grad is None else grad + g
            out[block_at(order_ref[j], width), :] = grad.astype(BF)

    flops = 2 * cap * width * len(keys) * hidden
    outs = [shaped(width * len(keys), hidden, dtype=BF)]
    return call(kernel, "grads_in", flops, outs, [order], *[[x] for x in xs], pre_grad)[0]


def grads_out(order, blocks, keys, gated):
    spots, ys = flat(blocks, keys)
    cap, width = blocks[0][0][1].shape
    hidden = gated.shape[1]

    def kernel(order_ref, *refs):
        ins, (hg_ref, out) = refs[: len(ys)], refs[len(ys) :]
        for j in range(len(keys)):
            grad = None
            for (k, at, rows), y in zip(spots, ins):
                if k == j:
                    g = dot(hg_ref[at : at + rows, :], y[...], 0, 0)
                    grad = g if grad is None else grad + g
            out[:, block_at(order_ref[j], width)] = grad.astype(BF)

    flops = 2 * cap * width * len(keys) * hidden
    outs = [shaped(hidden, width * len(keys), dtype=BF)]
    return call(kernel, "grads_out", flops, outs, [order], *ys, gated)[0]


def numbers(values):
    return jnp.stack(values).astype(jnp.int32)


def body(tokens, cotangent, w_in, w_out, router, chosen):
    planes = lax.axis_size("plane")
    slots = 2 * lax.axis_size("tensor")
    tok_dev, features = tokens.shape
    width = features // slots
    cap = chosen.shape[1]
    plane = lax.axis_index("plane")
    half = lax.axis_index("half")
    slot = lax.axis_index("tensor") * 2 + half
    homes = 2 * planes
    bucket = 4 * tok_dev // homes
    expert = plane.astype(jnp.int32)[None]
    router_row = lax.dynamic_slice_in_dim(router.T, plane, 1, 0).astype(F32)
    masks = chip_masks(slots)
    first = ((plane * 2 + half) * tok_dev).astype(jnp.int32)
    before_me = jnp.sum((chosen < first).astype(jnp.int32), axis=1)
    firsts = jnp.concatenate([first[None], before_me])
    chosen_cols = jnp.pad(chosen.T, ((0, bucket), (0, 0)), constant_values=-1)
    mine = lax.dynamic_slice_in_dim(chosen, plane, 1, 0)
    edges = jnp.arange(homes, dtype=jnp.int32)[:, None] * tok_dev
    reach = jnp.sum((mine < edges).astype(jnp.int32), axis=1)

    def tensor_slice(source):
        return lax.dynamic_slice_in_dim(source, (slot // 2) * 2 * width, 2 * width, 1)

    def exchange(x):
        return lax.all_to_all(x, ("plane", "half"), split_axis=0, concat_axis=0, tiled=True)

    def order_of(*keys):
        return numbers([slot ^ m for m in keys])

    x_sent, hots = pack(firsts, chosen_cols, tensor_slice(tokens), bucket)
    x_got = exchange(x_sent)
    w_in, w_out, _ = join(w_in, w_out, x_sent)
    w_in, w_out = stage(w_in, w_out)
    y_sent, _ = pack(firsts, chosen_cols, tensor_slice(cotangent), bucket)
    x_got, y_sent, w_in, w_out = join(x_got, y_sent, w_in, w_out)
    y_got = exchange(y_sent)
    xs = plane_gather(compact(reach, x_got, cap), slots)
    pieces = [x for m in xs for _, x in xs[m]]
    y_got, *pieces = join(y_got, *pieces)
    xs = {m: [(at, pieces.pop(0)) for at, _ in xs[m]] for m in xs}
    late = [m for m in masks if m.bit_count() > 1]
    late += [m | CORE for m in late]
    early = [m for m in xs if m not in late]
    keys = early + late
    order = order_of(*keys)
    pre_act, gate = project_in(order, expert, xs, keys, w_in, router)
    ys = plane_gather(compact(reach, y_got, cap), slots, pre_act)
    upstream = project_out(order_of(*early), ys, early, w_out)

    groups = [[m for m in masks if m.bit_count() > 1], [m for m in masks if m.bit_count() <= 1]]
    groups = [g[::-1] for g in groups]
    sizes = [len(g) for g in groups]
    near = [m for g in groups for m in g]
    gated, pre_grad, score_grad, far1, far2, near1, near2 = activation(
        order_of(*late, *[m | CORE for m in near], *near),
        ys,
        late,
        sizes,
        sizes,
        w_out,
        w_in,
        router_row,
        upstream,
        pre_act,
        gate,
    )
    hops = [
        lambda x, step=1 << i: lax.ppermute(x, "plane", [(e, e ^ step) for e in range(planes)])
        for i in range(planes.bit_length() - 1)
    ]
    hops += [functools.partial(flip, bit=1 << i) for i in reversed(range(slots.bit_length() - 1))]

    def hop(total):
        return total + hops.pop(0)(total) if hops else total

    mid = cap // 2
    got1, got2 = flip(far1, CORE), flip(far2, CORE)
    column = router_column(order, xs, keys, score_grad)
    got1, got2, column = join(got1, got2, column)
    total = jnp.where(jnp.arange(planes)[:, None] == plane, column, 0.0)
    sums = {m: near1[k] + got1[k].astype(F32) for k, m in enumerate(groups[0])}
    sums.update({m: near2[k] + got2[k].astype(F32) for k, m in enumerate(groups[1])})
    total = hop(total)
    for m in groups[0]:
        low, high = m & -m, top_bit(m)
        a, b = flip(sums[m][:mid].astype(BF), low), flip(sums[m][mid:].astype(BF), high)
        a, b, total, *rest = join(a, b, total, *[sums[k] for k in groups[1]])
        sums.update(zip(groups[1], rest))
        pad = jnp.zeros((cap - mid, width), F32)
        sums[m ^ low] = sums[m ^ low] + jnp.concatenate([a.astype(F32), pad])
        sums[m ^ high] = sums[m ^ high] + jnp.concatenate([pad, b.astype(F32)])
    sent = [sums[m].astype(BF) for m in groups[1] if m]
    *sent, total, pre_grad = join(*sent, total, pre_grad)
    came = [flip(x, m) for x, m in zip(sent, groups[1])]
    grad_in = grads_in(order, xs, keys, pre_grad)
    total = hop(total)
    *terms, grad_in, total = join(sums[0], *came, grad_in, total)

    back = place(reach, homes, bucket, terms)
    returned = exchange(back)
    grad_out = grads_out(order, ys, keys, after(gated, back))
    total = after(total, grad_out)
    while hops:
        total = hop(total)
    returned, grad_out, total = join(returned, grad_out, total)
    return (combine(hots, returned), grad_in, grad_out, total.T)


def solution(mesh):
    planes = mesh.shape["expert"] // 2
    inner = Mesh(mesh.devices.reshape(planes, 2, mesh.shape["tensor"]), ("plane", "half", "tensor"))
    home = ("plane", "half")
    every = ("plane", "half", "tensor")
    return jax.shard_map(
        body,
        mesh=inner,
        in_specs=(P(home, None), P(home, None), P(None, every), P(every, None), P(), P()),
        out_specs=(P(home, "tensor"), P(None, every), P(every, None), P()),
        check_vma=False,
    )
```

```python
import functools
import math

import jax
import jax.numpy as jnp
from jax import lax
from jax.experimental import pallas as pl
from jax.experimental.pallas import tpu as pltpu
from jax.sharding import Mesh
from jax.sharding import PartitionSpec as P

BF = jnp.bfloat16
F32 = jnp.float32
CORE = 2
VMEM_LIMIT = 24 * 1024 * 1024


def dot(a, b, da, db):
    return lax.dot_general(a, b, (((da,), (db,)), ((), ())), preferred_element_type=F32)


def flip(x, bit):
    if bit == 1:
        return lax.ppermute(x, "half", [(0, 1), (1, 0)])
    n = lax.axis_size("tensor")
    return lax.ppermute(x, "tensor", [(i, i ^ (bit >> 1)) for i in range(n)])


def chip_masks(slots):
    return sorted((m for m in range(slots) if not m & CORE), key=lambda m: (m.bit_count(), m))


def top_bit(m):
    return 1 << (m.bit_length() - 1)


def plane_gather(own, slots, *before):
    half = own.shape[0] // 2
    blocks = {0: [(0, own)]}
    for m in chip_masks(slots)[1:]:
        low, high = m & -m, top_bit(m)
        if low == high:
            blocks[m] = [(0, flip(own, m))]
        else:
            first = rows_of(blocks[m ^ low], 0, half)
            second = rows_of(blocks[m ^ high], half, half)
            if before:
                first, second = after(first, *before), after(second, *before)
            blocks[m] = [(0, flip(first, low)), (half, flip(second, high))]
    return blocks


def add_core(blocks, masks):
    for m in masks:
        blocks[m | CORE] = [(at, flip(x, CORE)) for at, x in blocks[m]]


def rows_of(pieces, start, count):
    for at, x in pieces:
        if at == start and x.shape[0] == count:
            return x
        if at <= start and start + count <= at + x.shape[0]:
            return x[start - at : start - at + count]
    raise ValueError("rows split")


def after(x, *others):
    return lax.optimization_barrier((x, *others))[0]


def join(*arrays):
    return lax.optimization_barrier(arrays)


class Tiles:
    def __init__(self, x, axis, count, first=0):
        self.x, self.axis, self.count, self.first = x, axis, count, first
        self.size = x.shape[axis] // (2 * lax.axis_size("tensor"))

    def at(self, ref, order_ref, j):
        here = block_at(order_ref[self.first + j], self.size)
        return ref.at[here, :] if self.axis == 0 else ref.at[:, here]


def call(kernel, name, flops, outs, smem, *args):
    flat_args = list(smem)
    for x in args:
        if isinstance(x, Tiles):
            x = x.x
        elif isinstance(x, list):
            x = pltpu.with_memory_space_constraint(x[0], pltpu.HBM)
        flat_args.append(x)

    def run(*refs):
        scalars, refs = refs[: len(smem)], list(refs[len(smem) :])
        for i, x in enumerate(args):
            if isinstance(x, Tiles):
                refs[i] = [x.at(refs[i], scalars[0], j) for j in range(x.count)]
        kernel(*scalars, *refs)

    moved = sum(a.size * a.dtype.itemsize for a in flat_args) + 4 * sum(math.prod(o.shape) for o in outs)
    return pl.pallas_call(
        run,
        in_specs=[pl.BlockSpec(memory_space=pltpu.SMEM)] * len(smem)
        + [pl.BlockSpec(memory_space=pltpu.VMEM)] * len(args),
        out_specs=[pl.BlockSpec(memory_space=pltpu.VMEM)] * len(outs),
        out_shape=outs,
        compiler_params=pltpu.CompilerParams(vmem_limit_bytes=VMEM_LIMIT),
        cost_estimate=pl.CostEstimate(flops=int(flops), bytes_accessed=int(moved), transcendentals=0),
        name=name,
    )(*flat_args)


def shaped(*shape, dtype=F32):
    return jax.ShapeDtypeStruct(shape, dtype)


def block_at(start, size):
    return pl.ds(pl.multiple_of(start * size, size), size)


def pack(firsts, chosen, sources, bucket, halves):
    experts, cap = chosen.shape
    rows, width = sources[0].shape

    def kernel(firsts_ref, chosen_ref, *refs):
        ins, (out, hot_out) = refs[: len(sources)], refs[len(sources) :]
        for e in range(experts):
            line = chosen_ref[e : e + 1, :]
            start = jnp.sum((line < firsts_ref[0]).astype(jnp.int32))
            line = pltpu.roll(jnp.broadcast_to(line, (8, cap)), cap - start, 1)[:1, :bucket]
            got = None
            for i, x in enumerate(ins):
                hot = lax.broadcasted_iota(jnp.int32, (rows, bucket), 0) == line - firsts_ref[i + 1]
                hot = hot.astype(F32).astype(BF)
                hot_out[e] = hot
                term = dot(hot, x[...], 0, 0)
                got = term if got is None else got + term
            got = got.astype(BF)
            if halves:
                out[2 * e], out[2 * e + 1] = got[:, : width // 2], got[:, width // 2 :]
            else:
                out[e] = got

    flops = 2 * experts * bucket * rows * width * len(sources)
    cut = 2 if halves else 1
    outs = [
        shaped(experts * cut, bucket, width // cut, dtype=BF),
        pltpu.HBM((experts, rows, bucket), BF),
    ]
    return call(kernel, "pack_rows", flops, outs, [firsts], chosen, *sources)


def compact(reach, buckets, cap):
    homes, bucket, width = buckets.shape

    def kernel(reach_ref, buckets_ref, out):
        acc = None
        for s in range(homes):
            at = lax.broadcasted_iota(jnp.int32, (cap, bucket), 0) - reach_ref[s]
            hot = lax.broadcasted_iota(jnp.int32, (cap, bucket), 1) == at
            term = dot(hot.astype(F32).astype(BF), buckets_ref[s], 1, 0)
            acc = term if acc is None else acc + term
        out[...] = acc.astype(BF)

    flops = 2 * cap * homes * bucket * width
    outs = [shaped(cap, width, dtype=BF)]
    return call(kernel, "compact_rows", flops, outs, [reach], buckets)[0]


def place(reach, homes, bucket, terms):
    cap, width = terms[0].shape

    def kernel(reach_ref, *refs):
        total = refs[0][...].astype(F32)
        for r in refs[1:-1]:
            total = total + r[...].astype(F32)
        rows = total.astype(BF)
        for s in range(homes):
            at = lax.broadcasted_iota(jnp.int32, (bucket, cap), 1) - reach_ref[s]
            hot = lax.broadcasted_iota(jnp.int32, (bucket, cap), 0) == at
            refs[-1][s] = dot(hot.astype(F32).astype(BF), rows, 1, 0).astype(BF)

    flops = 2 * cap * homes * bucket * width
    outs = [shaped(homes, bucket, width, dtype=BF)]
    return call(kernel, "place_rows", flops, outs, [reach], *terms)[0]


def combine(hots, returned):
    experts, rows, bucket = hots.shape
    width = returned.shape[2]

    def kernel(hots_ref, returned_ref, out):
        for h in range(2):
            acc = None
            for e in range(experts):
                term = dot(hots_ref[e], returned_ref[2 * e + h], 1, 0)
                acc = term if acc is None else acc + term
            out[:, h * width : (h + 1) * width] = acc.astype(BF)

    flops = 4 * experts * bucket * rows * width
    outs = [shaped(rows, 2 * width, dtype=BF)]
    return call(kernel, "combine_rows", flops, outs, [], hots, returned)[0]


def flat(blocks, keys):
    spots = [(j, at, x.shape[0]) for j, m in enumerate(keys) for at, x in blocks[m]]
    return spots, [x for m in keys for _, x in blocks[m]]


def add_rows(total, at, rows, values):
    done = []
    for start, old in total:
        size = old.shape[0]
        if at <= start and start + size <= at + rows:
            done.append((start, old + values[start - at : start - at + size]))
        elif start <= at and at + rows <= start + size:
            cuts = [(start, old[: at - start]), (at, old[at - start : at - start + rows] + values)]
            cuts.append((at + rows, old[at - start + rows :]))
            done += [c for c in cuts if c[1].shape[0]]
        else:
            done.append((start, old))
    return done


def product(spots, ins, tiles, side):
    total = None
    for (j, at, rows), x in zip(spots, ins):
        term = dot(x[...], tiles[j][...], 1, side)
        total = [(at, term)] if total is None else add_rows(total, at, rows, term)
    return total


def project_in(order, expert, blocks, keys, w_in, router):
    spots, xs = flat(blocks, keys)
    cap, width = blocks[0][0][1].shape
    hidden = w_in.shape[1]
    experts = router.shape[0]

    def kernel(order_ref, expert_ref, *refs):
        ins, (tiles, r_ref, a_ref, gate_ref) = refs[: len(xs)], refs[len(xs) :]
        scores = None
        for (j, at, rows), x in zip(spots, ins):
            s = dot(x[...], r_ref[:, block_at(order_ref[j], width)], 1, 1)
            scores = [(at, s)] if scores is None else add_rows(scores, at, rows, s)
            a = dot(x[...], tiles[j][...], 1, 0)
            if j == 0:
                a_ref[at : at + rows, :] = a
            else:
                a_ref[at : at + rows, :] += a
        for at, s in scores:
            mine = lax.broadcasted_iota(jnp.int32, s.shape, 1) == expert_ref[0]
            picked = jnp.sum(jnp.where(mine, s, 0.0), axis=1, keepdims=True)
            gate_ref[at : at + s.shape[0], :] = jax.nn.sigmoid(picked)

    flops = 2 * cap * width * len(keys) * hidden
    outs = [shaped(cap, hidden), shaped(cap, 1)]
    tiles = Tiles(w_in, 0, len(keys))
    return call(kernel, "project_in", flops, outs, [order, expert], *[[x] for x in xs], tiles, router)


def project_out(order, blocks, keys, w_out):
    spots, ys = flat(blocks, keys)
    cap, width = blocks[0][0][1].shape
    hidden = w_out.shape[0]

    def kernel(order_ref, *refs):
        ins, (w_ref, up) = refs[: len(ys)], refs[len(ys) :]
        for (j, at, rows), y in zip(spots, ins):
            u = dot(y[...], w_ref[:, block_at(order_ref[j], width)], 1, 1)
            if j == 0:
                up[at : at + rows, :] = u
            else:
                up[at : at + rows, :] += u

    flops = 2 * cap * width * len(keys) * hidden
    return call(kernel, "project_out", flops, [shaped(cap, hidden)], [order], *ys, [w_out])[0]


def activation(order, blocks, keys, far, near, tiles, w_in, router_row, upstream, pre_act, gate):
    spots, ys = flat(blocks, keys)
    width = blocks[0][0][1].shape[1]
    cap, hidden = pre_act.shape
    count = sum(far) + sum(near)

    def kernel(order_ref, *refs):
        ins, refs = refs[: len(ys)], refs[len(ys) :]
        late, refs = refs[: len(tiles)], refs[len(tiles) :]
        back, r_ref, u_ref, a_ref, gate_ref, hg_ref, da_ref, ds_ref, *outs = refs
        up = [(0, u_ref[...])]
        for (j, at, rows), y in zip(spots, ins):
            up = add_rows(up, at, rows, dot(y[...], late[j][...], 1, 1))
        for at, u in up:
            place = slice(at, at + u.shape[0])
            a = a_ref[place, :]
            gate = gate_ref[place, :]
            sig = jax.nn.sigmoid(a)
            act = a * sig
            hg_ref[place, :] = (gate * act).astype(BF)
            gate_grad = jnp.sum(act * u, axis=1, keepdims=True)
            ds_ref[place, :] = gate_grad * gate * (1.0 - gate)
            da_ref[place, :] = (gate * u * sig * (1.0 + a * (1.0 - sig))).astype(BF)
        places = [(out, k) for out, n in zip(outs, far + near) for k in range(n)]
        for k, (out, spot) in enumerate(places):
            here = block_at(order_ref[k], width)
            block = dot(da_ref[...], back[k][...], 1, 1) + ds_ref[...] * r_ref[:, here]
            out[spot] = block.astype(out.dtype)

    flops = 2 * cap * width * (len(keys) + count) * hidden
    outs = [shaped(cap, hidden, dtype=BF), shaped(cap, hidden, dtype=BF), shaped(cap, 1)]
    outs += [shaped(n, cap, width, dtype=BF) for n in far] + [shaped(n, cap, width) for n in near]
    more = (Tiles(w_in, 0, count), router_row, upstream, pre_act, gate)
    return call(kernel, "activation", flops, outs, [order], *ys, *tiles, *more)


def router_column(order, blocks, keys, score_grad):
    spots, xs = flat(blocks, keys)
    width = blocks[0][0][1].shape[1]

    def kernel(order_ref, *refs):
        ins, (ds_ref, col) = refs[: len(xs)], refs[len(xs) :]
        for j in range(len(keys)):
            line = None
            for (k, at, rows), x in zip(spots, ins):
                if k == j:
                    c = jnp.sum(x[...].astype(F32) * ds_ref[at : at + rows, :], axis=0, keepdims=True)
                    line = c if line is None else line + c
            col[:, block_at(order_ref[j], width)] = line

    flops = 2 * score_grad.shape[0] * width * len(keys)
    outs = [shaped(1, width * len(keys))]
    return call(kernel, "router_column", flops, outs, [order], *[[x] for x in xs], score_grad)[0]


def grads_in(order, blocks, keys, pre_grad):
    spots, xs = flat(blocks, keys)
    cap, width = blocks[0][0][1].shape
    hidden = pre_grad.shape[1]

    def kernel(order_ref, *refs):
        ins, (da_ref, out) = refs[: len(xs)], refs[len(xs) :]
        for j in range(len(keys)):
            grad = None
            for (k, at, rows), x in zip(spots, ins):
                if k == j:
                    g = dot(x[...], da_ref[at : at + rows, :], 0, 0)
                    grad = g if grad is None else grad + g
            out[block_at(order_ref[j], width), :] = grad.astype(BF)

    flops = 2 * cap * width * len(keys) * hidden
    outs = [shaped(width * len(keys), hidden, dtype=BF)]
    return call(kernel, "grads_in", flops, outs, [order], *[[x] for x in xs], pre_grad)[0]


def grads_out(order, blocks, keys, gated):
    spots, ys = flat(blocks, keys)
    cap, width = blocks[0][0][1].shape
    hidden = gated.shape[1]

    def kernel(order_ref, *refs):
        ins, (hg_ref, out) = refs[: len(ys)], refs[len(ys) :]
        for j in range(len(keys)):
            grad = None
            for (k, at, rows), y in zip(spots, ins):
                if k == j:
                    g = dot(hg_ref[at : at + rows, :], y[...], 0, 0)
                    grad = g if grad is None else grad + g
            out[:, block_at(order_ref[j], width)] = grad.astype(BF)

    flops = 2 * cap * width * len(keys) * hidden
    outs = [shaped(hidden, width * len(keys), dtype=BF)]
    return call(kernel, "grads_out", flops, outs, [order], *[[y] for y in ys], gated)[0]


def numbers(values):
    return jnp.stack(values).astype(jnp.int32)


def body(tokens, cotangent, w_in, w_out, router, chosen):
    planes = lax.axis_size("plane")
    slots = 2 * lax.axis_size("tensor")
    tok_dev, features = tokens.shape
    width = features // slots
    cap = chosen.shape[1]
    plane = lax.axis_index("plane")
    half = lax.axis_index("half")
    slot = lax.axis_index("tensor") * 2 + half
    homes = 2 * planes
    bucket = 4 * tok_dev // homes
    expert = plane.astype(jnp.int32)[None]
    router_row = lax.dynamic_slice_in_dim(router.T, plane, 1, 0).astype(F32)
    masks = chip_masks(slots)
    firsts = numbers([(plane * 2 + half) * tok_dev] * 2)
    plane_firsts = numbers([(plane * 2 + part) * tok_dev for part in (0, half, 1 - half)])
    mine = lax.dynamic_slice_in_dim(chosen, plane, 1, 0)
    edges = jnp.arange(homes, dtype=jnp.int32)[:, None] * tok_dev
    reach = jnp.sum((mine < edges).astype(jnp.int32), axis=1)

    def columns(source, start, count):
        return lax.dynamic_slice_in_dim(source, start * width, count * width, 1)

    def exchange(x, axes):
        return lax.all_to_all(x, axes, split_axis=0, concat_axis=0, tiled=True)

    def order_of(*keys):
        return numbers([slot ^ m for m in keys])

    late = [m for m in masks if m.bit_count() > 1]
    early = [m for m in masks if m not in late]
    late_keys = late + [m | CORE for m in late]
    early_keys = early + [m | CORE for m in early]
    keys = early_keys + late_keys
    order = order_of(*keys)

    x_sent, hots = pack(firsts, chosen, [columns(tokens, slot // 2 * 2, 2)], bucket, True)
    x_got = exchange(x_sent, ("plane", "half"))
    cotangent, w_out, _ = join(cotangent, w_out, x_sent)
    y_own, y_away = columns(cotangent, slot, 1), flip(columns(cotangent, slot ^ 1, 1), 1)
    y_sent, _ = pack(plane_firsts, chosen, [y_own, y_away], 2 * bucket, False)
    tiles = [columns(w_out, slot ^ m, 1) for m in late_keys]
    x_got, y_sent, *tiles = join(x_got, y_sent, *tiles)

    y_got = exchange(y_sent, "plane")
    xs = plane_gather(compact(reach, x_got, cap), slots)
    add_core(xs, masks)
    pieces = [x for m in xs for _, x in xs[m]]
    y_got, *pieces = join(y_got, *pieces)
    xs = {m: [(at, pieces.pop(0)) for at, _ in xs[m]] for m in xs}

    pre_act, gate = project_in(order, expert, xs, keys, w_in, router.T)
    ys = plane_gather(compact(reach[::2], y_got, cap), slots, pre_act)
    tied = {m: [(at, after(x, pre_act)) for at, x in ys[m]] for m in early}
    add_core(tied, early)
    ys.update({m: tied[m] for m in tied if m & CORE})
    upstream = project_out(order_of(*early_keys), ys, early_keys, w_out)
    for m in late:
        ys[m] = [(at, after(x, upstream)) for at, x in ys[m]]
    add_core(ys, late)

    groups = [late[::-1], early[::-1]]
    sizes = [len(g) for g in groups]
    near = [m for g in groups for m in g]
    gated, pre_grad, score_grad, far1, far2, near1, near2 = activation(
        order_of(*[m | CORE for m in near], *near),
        ys,
        late_keys,
        sizes,
        sizes,
        tiles,
        w_in,
        router_row,
        upstream,
        pre_act,
        gate,
    )
    hops = [
        lambda x, step=1 << i: lax.ppermute(x, "plane", [(e, e ^ step) for e in range(planes)])
        for i in range(planes.bit_length() - 1)
    ]
    hops += [functools.partial(flip, bit=1 << i) for i in reversed(range(slots.bit_length() - 1))]

    def hop(total):
        return total + hops.pop(0)(total) if hops else total

    mid = cap // 2
    got1, got2 = flip(far1, CORE), flip(far2, CORE)
    column = router_column(order, xs, keys, score_grad)
    got1, got2, column = join(got1, got2, column)
    total = jnp.where(jnp.arange(planes)[:, None] == plane, column, 0.0)
    sums = {m: near1[k] + got1[k].astype(F32) for k, m in enumerate(groups[0])}
    sums.update({m: near2[k] + got2[k].astype(F32) for k, m in enumerate(groups[1])})
    total = hop(total)
    for m in groups[0]:
        low, high = m & -m, top_bit(m)
        a, b = flip(sums[m][:mid].astype(BF), low), flip(sums[m][mid:].astype(BF), high)
        a, b, total, *rest = join(a, b, total, *[sums[k] for k in groups[1]])
        sums.update(zip(groups[1], rest))
        pad = jnp.zeros((cap - mid, width), F32)
        sums[m ^ low] = sums[m ^ low] + jnp.concatenate([a.astype(F32), pad])
        sums[m ^ high] = sums[m ^ high] + jnp.concatenate([pad, b.astype(F32)])
    sent = [sums[m].astype(BF) for m in groups[1] if m]
    *sent, total, pre_grad = join(*sent, total, pre_grad)
    came = [flip(x, m) for x, m in zip(sent, groups[1])]
    grad_in = grads_in(order, xs, keys, pre_grad)
    total = hop(total)
    *terms, grad_in, total = join(sums[0], *came, grad_in, total)

    back = place(reach, homes, bucket, terms)
    returned = exchange(back, ("plane", "half"))
    grad_out = grads_out(order, ys, keys, after(gated, back))
    total = after(total, grad_out)
    while hops:
        total = hop(total)
    returned, grad_out, total = join(returned, grad_out, total)
    return (combine(hots, returned), grad_in, grad_out, total.T)


def solution(mesh):
    planes = mesh.shape["expert"] // 2
    inner = Mesh(mesh.devices.reshape(planes, 2, mesh.shape["tensor"]), ("plane", "half", "tensor"))
    home = ("plane", "half")
    every = ("plane", "half", "tensor")
    return jax.shard_map(
        body,
        mesh=inner,
        in_specs=(P(home, None), P(home, None), P(None, every), P(every, None), P(), P()),
        out_specs=(P(home, "tensor"), P(None, every), P(every, None), P()),
        check_vma=False,
    )
```

```python
import functools
import math

import jax
import jax.numpy as jnp
from jax import lax
from jax.experimental import pallas as pl
from jax.experimental.pallas import tpu as pltpu
from jax.sharding import Mesh
from jax.sharding import PartitionSpec as P

BF = jnp.bfloat16
F32 = jnp.float32
CORE = 2
VMEM_LIMIT = 24 * 1024 * 1024


def dot(a, b, da, db):
    return lax.dot_general(a, b, (((da,), (db,)), ((), ())), preferred_element_type=F32)


def flip(x, bit):
    if bit == 1:
        return lax.ppermute(x, "half", [(0, 1), (1, 0)])
    n = lax.axis_size("tensor")
    return lax.ppermute(x, "tensor", [(i, i ^ (bit >> 1)) for i in range(n)])


def chip_masks(slots):
    return sorted((m for m in range(slots) if not m & CORE), key=lambda m: (m.bit_count(), m))


def top_bit(m):
    return 1 << (m.bit_length() - 1)


def plane_gather(top, bottom, slots):
    half = top.shape[0]
    blocks = {0: [(0, top), (half, bottom)]}
    for m in chip_masks(slots)[1:]:
        low, high = m & -m, top_bit(m)
        first, second = (blocks[0], blocks[0]) if low == high else (blocks[m ^ low], blocks[m ^ high])
        blocks[m] = [(0, flip(first[0][1], low)), (half, flip(second[1][1], high))]
    return blocks


def add_core(blocks, masks):
    for m in masks:
        blocks[m | CORE] = [(at, flip(x, CORE)) for at, x in blocks[m]]


def after(x, *others):
    return lax.optimization_barrier((x, *others))[0]


def join(*arrays):
    return lax.optimization_barrier(arrays)


def in_hbm(x):
    return pltpu.with_memory_space_constraint(x, pltpu.HBM)


class Tiles:
    def __init__(self, x, axis, count, hbm=False):
        self.x, self.axis, self.count = x, axis, count
        if hbm:
            self.x = in_hbm(x)
        self.size = x.shape[axis] // (2 * lax.axis_size("tensor"))

    def at(self, ref, order_ref, j):
        here = block_at(order_ref[j], self.size)
        return ref.at[here, :] if self.axis == 0 else ref.at[:, here]


def call(kernel, name, flops, outs, smem, *args):
    flat_args = list(smem)
    for x in args:
        if isinstance(x, Tiles):
            x = x.x
        elif isinstance(x, list):
            x = in_hbm(x[0])
        flat_args.append(x)

    def run(*refs):
        scalars, refs = refs[: len(smem)], list(refs[len(smem) :])
        for i, x in enumerate(args):
            if isinstance(x, Tiles):
                refs[i] = [x.at(refs[i], scalars[0], j) for j in range(x.count)]
        kernel(*scalars, *refs)

    moved = sum(a.size * a.dtype.itemsize for a in flat_args) + 4 * sum(math.prod(o.shape) for o in outs)
    return pl.pallas_call(
        run,
        in_specs=[pl.BlockSpec(memory_space=pltpu.SMEM)] * len(smem)
        + [pl.BlockSpec(memory_space=pltpu.VMEM)] * len(args),
        out_specs=[pl.BlockSpec(memory_space=pltpu.VMEM)] * len(outs),
        out_shape=outs,
        compiler_params=pltpu.CompilerParams(vmem_limit_bytes=VMEM_LIMIT),
        cost_estimate=pl.CostEstimate(flops=int(flops), bytes_accessed=int(moved), transcendentals=0),
        name=name,
    )(*flat_args)


def shaped(*shape, dtype=F32):
    return jax.ShapeDtypeStruct(shape, dtype)


def block_at(start, size):
    return pl.ds(pl.multiple_of(start * size, size), size)


def pack(firsts, chosen, sources, bucket, halves):
    experts, cap = chosen.shape
    rows, width = sources[0].shape

    def kernel(firsts_ref, chosen_ref, *refs):
        ins, (out, hot_out) = refs[: len(sources)], refs[len(sources) :]
        for e in range(experts):
            line = chosen_ref[e : e + 1, :]
            start = jnp.sum((line < firsts_ref[0]).astype(jnp.int32))
            line = pltpu.roll(jnp.broadcast_to(line, (8, cap)), cap - start, 1)[:1, :bucket]
            got = None
            for i, x in enumerate(ins):
                hot = lax.broadcasted_iota(jnp.int32, (rows, bucket), 0) == line - firsts_ref[i + 1]
                hot = hot.astype(F32).astype(BF)
                hot_out[e] = hot
                term = dot(hot, x[...], 0, 0)
                got = term if got is None else got + term
            got = got.astype(BF)
            if halves:
                out[2 * e], out[2 * e + 1] = got[:, : width // 2], got[:, width // 2 :]
            else:
                out[e] = got

    flops = 2 * experts * bucket * rows * width * len(sources)
    parts = 2 if halves else 1
    outs = [
        pltpu.HBM((experts * parts, bucket, width // parts), BF),
        pltpu.HBM((experts, rows, bucket), BF),
    ]
    return call(kernel, "pack_rows", flops, outs, [firsts], chosen, *sources)


def compact(reach, buckets, cap):
    homes, bucket, width = buckets.shape

    def kernel(reach_ref, buckets_ref, top, bottom):
        acc = None
        for s in range(homes):
            at = lax.broadcasted_iota(jnp.int32, (cap, bucket), 0) - reach_ref[s]
            hot = lax.broadcasted_iota(jnp.int32, (cap, bucket), 1) == at
            term = dot(hot.astype(F32).astype(BF), buckets_ref[s], 1, 0)
            acc = term if acc is None else acc + term
        top[...], bottom[...] = acc[: cap // 2].astype(BF), acc[cap // 2 :].astype(BF)

    flops = 2 * cap * homes * bucket * width
    outs = [shaped(cap // 2, width, dtype=BF)] * 2
    return call(kernel, "compact_rows", flops, outs, [reach], buckets)


def place(reach, homes, bucket, terms):
    cap, width = terms[0].shape

    def kernel(reach_ref, *refs):
        total = refs[0][...].astype(F32)
        for r in refs[1:-1]:
            total = total + r[...].astype(F32)
        rows = total.astype(BF)
        for s in range(homes):
            at = lax.broadcasted_iota(jnp.int32, (bucket, cap), 1) - reach_ref[s]
            hot = lax.broadcasted_iota(jnp.int32, (bucket, cap), 0) == at
            refs[-1][s] = dot(hot.astype(F32).astype(BF), rows, 1, 0).astype(BF)

    flops = 2 * cap * homes * bucket * width
    outs = [shaped(homes, bucket, width, dtype=BF)]
    return call(kernel, "place_rows", flops, outs, [reach], *terms)[0]


def combine(hots, returned):
    experts, rows, bucket = hots.shape
    width = returned.shape[2]

    def kernel(hots_ref, returned_ref, out):
        for h in range(2):
            acc = None
            for e in range(experts):
                term = dot(hots_ref[e], returned_ref[2 * e + h], 1, 0)
                acc = term if acc is None else acc + term
            out[:, h * width : (h + 1) * width] = acc.astype(BF)

    flops = 4 * experts * bucket * rows * width
    outs = [shaped(rows, 2 * width, dtype=BF)]
    return call(kernel, "combine_rows", flops, outs, [], hots, returned)[0]


def flat(blocks, keys):
    spots = [(j, at, x.shape[0]) for j, m in enumerate(keys) for at, x in blocks[m]]
    return spots, [x for m in keys for _, x in blocks[m]]


def add_rows(total, at, rows, values):
    done = []
    for start, old in total:
        size = old.shape[0]
        if at <= start and start + size <= at + rows:
            done.append((start, old + values[start - at : start - at + size]))
        elif start <= at and at + rows <= start + size:
            cuts = [(start, old[: at - start]), (at, old[at - start : at - start + rows] + values)]
            cuts.append((at + rows, old[at - start + rows :]))
            done += [c for c in cuts if c[1].shape[0]]
        else:
            done.append((start, old))
    return done


def product(spots, ins, tiles, side):
    total = None
    for (j, at, rows), x in zip(spots, ins):
        term = dot(x[...], tiles[j][...], 1, side)
        total = [(at, term)] if total is None else add_rows(total, at, rows, term)
    return total


def project_in(order, expert, blocks, keys, w_in, router):
    spots, xs = flat(blocks, keys)
    cap, width = 2 * blocks[0][0][1].shape[0], blocks[0][0][1].shape[1]
    hidden = w_in.shape[1]
    experts = router.shape[0]

    def kernel(order_ref, expert_ref, *refs):
        ins, (tiles, r_ref, a_ref, gate_ref) = refs[: len(xs)], refs[len(xs) :]
        scores = {}
        for (j, at, rows), x in zip(spots, ins):
            s = dot(x[...], r_ref[:, block_at(order_ref[j], width)], 1, 1)
            scores[at] = scores[at] + s if at in scores else s
            a = dot(x[...], tiles[j][...], 1, 0)
            if j == 0:
                a_ref[at : at + rows, :] = a
            else:
                a_ref[at : at + rows, :] += a
        for at, s in scores.items():
            mine = lax.broadcasted_iota(jnp.int32, s.shape, 1) == expert_ref[0]
            picked = jnp.sum(jnp.where(mine, s, 0.0), axis=1, keepdims=True)
            gate_ref[at : at + s.shape[0], :] = jax.nn.sigmoid(picked)

    flops = 2 * cap * width * len(keys) * hidden
    outs = [shaped(cap, hidden), shaped(cap, 1)]
    tiles = Tiles(w_in, 0, len(keys), hbm=True)
    return call(kernel, "project_in", flops, outs, [order, expert], *[[x] for x in xs], tiles, router)


def project_out(order, blocks, keys, w_out):
    spots, ys = flat(blocks, keys)
    cap, width = 2 * blocks[0][0][1].shape[0], blocks[0][0][1].shape[1]
    hidden = w_out.shape[0]

    def kernel(order_ref, *refs):
        ins, (w_ref, up) = refs[: len(ys)], refs[len(ys) :]
        for (j, at, rows), y in zip(spots, ins):
            u = dot(y[...], w_ref[:, block_at(order_ref[j], width)], 1, 1)
            if j == 0:
                up[at : at + rows, :] = u
            else:
                up[at : at + rows, :] += u

    flops = 2 * cap * width * len(keys) * hidden
    return call(kernel, "project_out", flops, [shaped(cap, hidden)], [order], *ys, [w_out])[0]


def activation(order, blocks, keys, far, near, tiles, w_in, router_row, upstream, pre_act, gate):
    spots, ys = flat(blocks, keys)
    width = blocks[0][0][1].shape[1]
    cap, hidden = pre_act.shape
    count = sum(far) + sum(near)

    def kernel(order_ref, *refs):
        ins, refs = refs[: len(ys)], refs[len(ys) :]
        late, refs = refs[: len(tiles)], refs[len(tiles) :]
        back, r_ref, u_ref, a_ref, gate_ref, hg_ref, da_ref, ds_ref, *outs = refs
        up = [(0, u_ref[...])]
        for (j, at, rows), y in zip(spots, ins):
            up = add_rows(up, at, rows, dot(y[...], late[j][...], 1, 1))
        for at, u in up:
            place = slice(at, at + u.shape[0])
            a = a_ref[place, :]
            gate = gate_ref[place, :]
            sig = jax.nn.sigmoid(a)
            act = a * sig
            hg_ref[place, :] = (gate * act).astype(BF)
            gate_grad = jnp.sum(act * u, axis=1, keepdims=True)
            ds_ref[place, :] = gate_grad * gate * (1.0 - gate)
            da_ref[place, :] = (gate * u * sig * (1.0 + a * (1.0 - sig))).astype(BF)
        places = [(out, k) for out, n in zip(outs, far + near) for k in range(n)]
        for k, (out, spot) in enumerate(places):
            here = block_at(order_ref[k], width)
            block = dot(da_ref[...], back[k][...], 1, 1) + ds_ref[...] * r_ref[:, here]
            out[spot] = block.astype(out.dtype)

    flops = 2 * cap * width * (len(keys) + count) * hidden
    outs = [shaped(cap, hidden, dtype=BF), shaped(cap, hidden, dtype=BF), shaped(cap, 1)]
    outs += [shaped(n, cap, width, dtype=BF) for n in far] + [shaped(n, cap, width) for n in near]
    more = (Tiles(w_in, 0, count), router_row, upstream, pre_act, gate)
    return call(kernel, "activation", flops, outs, [order], *ys, *tiles, *more)


def router_column(order, blocks, keys, score_grad):
    spots, xs = flat(blocks, keys)
    width = blocks[0][0][1].shape[1]

    def kernel(order_ref, *refs):
        ins, (ds_ref, col) = refs[: len(xs)], refs[len(xs) :]
        for j in range(len(keys)):
            line = None
            for (k, at, rows), x in zip(spots, ins):
                if k == j:
                    c = jnp.sum(x[...].astype(F32) * ds_ref[at : at + rows, :], axis=0, keepdims=True)
                    line = c if line is None else line + c
            col[:, block_at(order_ref[j], width)] = line

    flops = 2 * score_grad.shape[0] * width * len(keys)
    outs = [shaped(1, width * len(keys))]
    return call(kernel, "router_column", flops, outs, [order], *[[x] for x in xs], score_grad)[0]


def grads_in(order, blocks, keys, pre_grad):
    spots, xs = flat(blocks, keys)
    cap, width = 2 * blocks[0][0][1].shape[0], blocks[0][0][1].shape[1]
    hidden = pre_grad.shape[1]

    def kernel(order_ref, *refs):
        ins, (da_ref, out) = refs[: len(xs)], refs[len(xs) :]
        for j in range(len(keys)):
            grad = None
            for (k, at, rows), x in zip(spots, ins):
                if k == j:
                    g = dot(x[...], da_ref[at : at + rows, :], 0, 0)
                    grad = g if grad is None else grad + g
            out[block_at(order_ref[j], width), :] = grad.astype(BF)

    flops = 2 * cap * width * len(keys) * hidden
    outs = [shaped(width * len(keys), hidden, dtype=BF)]
    return call(kernel, "grads_in", flops, outs, [order], *[[x] for x in xs], pre_grad)[0]


def grads_out(order, blocks, keys, gated):
    spots, ys = flat(blocks, keys)
    cap, width = 2 * blocks[0][0][1].shape[0], blocks[0][0][1].shape[1]
    hidden = gated.shape[1]

    def kernel(order_ref, *refs):
        ins, (hg_ref, out) = refs[: len(ys)], refs[len(ys) :]
        for j in range(len(keys)):
            grad = None
            for (k, at, rows), y in zip(spots, ins):
                if k == j:
                    g = dot(hg_ref[at : at + rows, :], y[...], 0, 0)
                    grad = g if grad is None else grad + g
            out[:, block_at(order_ref[j], width)] = grad.astype(BF)

    flops = 2 * cap * width * len(keys) * hidden
    outs = [shaped(hidden, width * len(keys), dtype=BF)]
    return call(kernel, "grads_out", flops, outs, [order], *[[y] for y in ys], gated)[0]


def numbers(values):
    return jnp.stack(values).astype(jnp.int32)


def body(tokens, cotangent, w_in, w_out, router, chosen):
    planes = lax.axis_size("plane")
    slots = 2 * lax.axis_size("tensor")
    tok_dev, features = tokens.shape
    width = features // slots
    cap = chosen.shape[1]
    plane = lax.axis_index("plane")
    half = lax.axis_index("half")
    slot = lax.axis_index("tensor") * 2 + half
    homes = 2 * planes
    bucket = 4 * tok_dev // homes
    expert = plane.astype(jnp.int32)[None]
    router_row = lax.dynamic_slice_in_dim(router.T, plane, 1, 0).astype(F32)
    masks = chip_masks(slots)
    firsts = numbers([(plane * 2 + half) * tok_dev] * 2)
    plane_firsts = numbers([(plane * 2 + part) * tok_dev for part in (0, half, 1 - half)])
    mine = lax.dynamic_slice_in_dim(chosen, plane, 1, 0)
    edges = jnp.arange(homes, dtype=jnp.int32)[:, None] * tok_dev
    reach = jnp.sum((mine < edges).astype(jnp.int32), axis=1)

    def columns(source, start, count):
        return lax.dynamic_slice_in_dim(source, start * width, count * width, 1)

    def exchange(x, axes):
        return lax.all_to_all(x, axes, split_axis=0, concat_axis=0, tiled=True)

    def order_of(*keys):
        return numbers([slot ^ m for m in keys])

    late = [m for m in masks if m.bit_count() > 1]
    early = [m for m in masks if m not in late]
    late_keys = late + [m | CORE for m in late]
    early_keys = early + [m | CORE for m in early]
    keys = early_keys + late_keys
    order = order_of(*keys)

    x_sent, hots = pack(firsts, chosen, [columns(tokens, slot // 2 * 2, 2)], bucket, True)
    x_got = exchange(x_sent, ("plane", "half"))
    cotangent, w_out, _ = join(cotangent, w_out, x_sent)
    y_own, y_away = columns(cotangent, slot, 1), flip(columns(cotangent, slot ^ 1, 1), 1)
    y_sent, _ = pack(plane_firsts, chosen, [y_own, y_away], 2 * bucket, False)
    tiles = [columns(w_out, slot ^ m, 1) for m in late_keys]
    x_got, y_sent, *tiles = join(x_got, y_sent, *tiles)

    y_got = exchange(y_sent, "plane")
    xs = plane_gather(*compact(reach, x_got, cap), slots)
    add_core(xs, early)
    pieces = [x for m in xs for _, x in xs[m]]
    y_got, *pieces = join(y_got, *pieces)
    xs = {m: [(at, pieces.pop(0)) for at, _ in xs[m]] for m in xs}
    add_core(xs, late)

    pre_act, gate = project_in(order, expert, xs, keys, w_in, router.T)
    ys = plane_gather(*compact(reach[::2], y_got, cap), slots)
    tied = {m: [(at, after(x, pre_act)) for at, x in ys[m]] for m in early}
    add_core(tied, early)
    ys.update({m: tied[m] for m in tied if m & CORE})
    upstream = project_out(order_of(*early_keys), ys, early_keys, w_out)
    for m in late:
        ys[m] = [(at, after(x, upstream)) for at, x in ys[m]]
    add_core(ys, late)

    groups = [late[::-1], early[::-1]]
    sizes = [len(g) for g in groups]
    near = [m for g in groups for m in g]
    gated, pre_grad, score_grad, far1, far2, near1, near2 = activation(
        order_of(*[m | CORE for m in near], *near),
        ys,
        late_keys,
        sizes,
        sizes,
        tiles,
        w_in,
        router_row,
        upstream,
        pre_act,
        gate,
    )
    hops = [
        lambda x, step=1 << i: lax.ppermute(x, "plane", [(e, e ^ step) for e in range(planes)])
        for i in range(planes.bit_length() - 1)
    ]
    hops += [functools.partial(flip, bit=1 << i) for i in reversed(range(slots.bit_length() - 1))]

    def hop(total):
        return total + hops.pop(0)(total) if hops else total

    mid = cap // 2
    got1 = flip(far1, CORE)
    got1, near1, score_grad, far2 = join(got1, near1, score_grad, far2)
    got2 = flip(far2, CORE)
    sums = {m: near1[k] + got1[k].astype(F32) for k, m in enumerate(groups[0])}
    column = router_column(order, xs, keys, score_grad)
    sums.update({m: near2[k] + got2[k].astype(F32) for k, m in enumerate(groups[1])})
    for m in groups[0]:
        low, high = m & -m, top_bit(m)
        a, b = flip(sums[m][:mid].astype(BF), low), flip(sums[m][mid:].astype(BF), high)
        a, b, column, *rest = join(a, b, column, *[sums[k] for k in groups[1]])
        sums.update(zip(groups[1], rest))
        pad = jnp.zeros((cap - mid, width), F32)
        sums[m ^ low] = sums[m ^ low] + jnp.concatenate([a.astype(F32), pad])
        sums[m ^ high] = sums[m ^ high] + jnp.concatenate([pad, b.astype(F32)])
    sent = [sums[m].astype(BF) for m in groups[1] if m]
    *sent, column, pre_grad = join(*sent, column, pre_grad)
    came = [flip(x, m) for x, m in zip(sent, groups[1])]
    total = jnp.where(jnp.arange(planes)[:, None] == plane, column, 0.0)
    total = hop(total)
    grad_in = grads_in(order, xs, keys, pre_grad)
    total = hop(total)
    *terms, grad_in, total = join(sums[0], *came, grad_in, total)

    back = place(reach, homes, bucket, terms)
    returned = exchange(back, ("plane", "half"))
    grad_out = grads_out(order, ys, keys, after(gated, back))
    total = after(total, grad_out)
    while hops:
        total = hop(total)
    returned, grad_out, total = join(returned, grad_out, total)
    return (combine(hots, returned), grad_in, grad_out, total.T)


def solution(mesh):
    planes = mesh.shape["expert"] // 2
    inner = Mesh(mesh.devices.reshape(planes, 2, mesh.shape["tensor"]), ("plane", "half", "tensor"))
    home = ("plane", "half")
    every = ("plane", "half", "tensor")
    return jax.shard_map(
        body,
        mesh=inner,
        in_specs=(P(home, None), P(home, None), P(None, every), P(every, None), P(), P()),
        out_specs=(P(home, "tensor"), P(None, every), P(every, None), P()),
        check_vma=False,
    )
```

```python
import functools
import math

import jax
import jax.numpy as jnp
from jax import lax
from jax.experimental import pallas as pl
from jax.experimental.pallas import tpu as pltpu
from jax.sharding import Mesh
from jax.sharding import PartitionSpec as P

BF = jnp.bfloat16
F32 = jnp.float32
CORE = 2
VMEM_LIMIT = 24 * 1024 * 1024


def dot(a, b, da, db):
    return lax.dot_general(a, b, (((da,), (db,)), ((), ())), preferred_element_type=F32)


def flip(x, bit):
    if bit == 1:
        return lax.ppermute(x, "half", [(0, 1), (1, 0)])
    n = lax.axis_size("tensor")
    return lax.ppermute(x, "tensor", [(i, i ^ (bit >> 1)) for i in range(n)])


def chip_masks(slots):
    return sorted((m for m in range(slots) if not m & CORE), key=lambda m: (m.bit_count(), m))


def top_bit(m):
    return 1 << (m.bit_length() - 1)


def plane_gather(top, bottom, slots):
    half = top.shape[0]
    blocks = {0: [(0, top), (half, bottom)]}
    for m in chip_masks(slots)[1:]:
        low, high = m & -m, top_bit(m)
        first, second = (blocks[0], blocks[0]) if low == high else (blocks[m ^ low], blocks[m ^ high])
        blocks[m] = [(0, flip(first[0][1], low)), (half, flip(second[1][1], high))]
    return blocks


def add_core(blocks, masks):
    for m in masks:
        blocks[m | CORE] = [(at, flip(x, CORE)) for at, x in blocks[m]]


def after(x, *others):
    return lax.optimization_barrier((x, *others))[0]


def join(*arrays):
    return lax.optimization_barrier(arrays)


def in_hbm(x):
    return pltpu.with_memory_space_constraint(x, pltpu.HBM)


class Tiles:
    def __init__(self, x, axis, count, hbm=False):
        self.x, self.axis, self.count = x, axis, count
        if hbm:
            self.x = in_hbm(x)
        self.size = x.shape[axis] // (2 * lax.axis_size("tensor"))

    def at(self, ref, order_ref, j):
        here = block_at(order_ref[j], self.size)
        return ref.at[here, :] if self.axis == 0 else ref.at[:, here]


def call(kernel, name, flops, outs, smem, *args):
    flat_args = list(smem)
    for x in args:
        if isinstance(x, Tiles):
            x = x.x
        elif isinstance(x, list):
            x = in_hbm(x[0])
        flat_args.append(x)

    def run(*refs):
        scalars, refs = refs[: len(smem)], list(refs[len(smem) :])
        for i, x in enumerate(args):
            if isinstance(x, Tiles):
                refs[i] = [x.at(refs[i], scalars[0], j) for j in range(x.count)]
        kernel(*scalars, *refs)

    moved = sum(a.size * a.dtype.itemsize for a in flat_args) + 4 * sum(math.prod(o.shape) for o in outs)
    return pl.pallas_call(
        run,
        in_specs=[pl.BlockSpec(memory_space=pltpu.SMEM)] * len(smem)
        + [pl.BlockSpec(memory_space=pltpu.VMEM)] * len(args),
        out_specs=[pl.BlockSpec(memory_space=pltpu.VMEM)] * len(outs),
        out_shape=outs,
        compiler_params=pltpu.CompilerParams(vmem_limit_bytes=VMEM_LIMIT),
        cost_estimate=pl.CostEstimate(flops=int(flops), bytes_accessed=int(moved), transcendentals=0),
        name=name,
    )(*flat_args)


def shaped(*shape, dtype=F32):
    return jax.ShapeDtypeStruct(shape, dtype)


def block_at(start, size):
    return pl.ds(pl.multiple_of(start * size, size), size)


def pack(firsts, chosen, sources, bucket, halves):
    experts, cap = chosen.shape
    rows, width = sources[0].shape

    def kernel(firsts_ref, chosen_ref, *refs):
        ins, (out, hot_out) = refs[: len(sources)], refs[len(sources) :]
        for e in range(experts):
            line = chosen_ref[e : e + 1, :]
            start = jnp.sum((line < firsts_ref[0]).astype(jnp.int32))
            line = pltpu.roll(jnp.broadcast_to(line, (8, cap)), cap - start, 1)[:1, :bucket]
            got = None
            for i, x in enumerate(ins):
                hot = lax.broadcasted_iota(jnp.int32, (rows, bucket), 0) == line - firsts_ref[i + 1]
                hot = hot.astype(F32).astype(BF)
                hot_out[e] = hot
                term = dot(hot, x[...], 0, 0)
                got = term if got is None else got + term
            got = got.astype(BF)
            if halves:
                out[2 * e], out[2 * e + 1] = got[:, : width // 2], got[:, width // 2 :]
            else:
                out[e] = got

    flops = 2 * experts * bucket * rows * width * len(sources)
    parts = 2 if halves else 1
    outs = [
        pltpu.HBM((experts * parts, bucket, width // parts), BF),
        pltpu.HBM((experts, rows, bucket), BF),
    ]
    return call(kernel, "pack_rows", flops, outs, [firsts], chosen, *sources)


def compact(reach, buckets, cap):
    homes, bucket, width = buckets.shape

    def kernel(reach_ref, buckets_ref, top, bottom):
        acc = None
        for s in range(homes):
            at = lax.broadcasted_iota(jnp.int32, (cap, bucket), 0) - reach_ref[s]
            hot = lax.broadcasted_iota(jnp.int32, (cap, bucket), 1) == at
            term = dot(hot.astype(F32).astype(BF), buckets_ref[s], 1, 0)
            acc = term if acc is None else acc + term
        top[...], bottom[...] = acc[: cap // 2].astype(BF), acc[cap // 2 :].astype(BF)

    flops = 2 * cap * homes * bucket * width
    outs = [shaped(cap // 2, width, dtype=BF)] * 2
    return call(kernel, "compact_rows", flops, outs, [reach], buckets)


def place(reach, homes, bucket, terms):
    cap, width = terms[0].shape

    def kernel(reach_ref, *refs):
        total = refs[0][...].astype(F32)
        for r in refs[1:-1]:
            total = total + r[...].astype(F32)
        rows = total.astype(BF)
        for s in range(homes):
            at = lax.broadcasted_iota(jnp.int32, (bucket, cap), 1) - reach_ref[s]
            hot = lax.broadcasted_iota(jnp.int32, (bucket, cap), 0) == at
            refs[-1][s] = dot(hot.astype(F32).astype(BF), rows, 1, 0).astype(BF)

    flops = 2 * cap * homes * bucket * width
    outs = [shaped(homes, bucket, width, dtype=BF)]
    return call(kernel, "place_rows", flops, outs, [reach], *terms)[0]


def combine(hots, returned):
    experts, rows, bucket = hots.shape
    width = returned.shape[2]

    def kernel(hots_ref, returned_ref, out):
        for h in range(2):
            acc = None
            for e in range(experts):
                term = dot(hots_ref[e], returned_ref[2 * e + h], 1, 0)
                acc = term if acc is None else acc + term
            out[:, h * width : (h + 1) * width] = acc.astype(BF)

    flops = 4 * experts * bucket * rows * width
    outs = [shaped(rows, 2 * width, dtype=BF)]
    return call(kernel, "combine_rows", flops, outs, [], hots, returned)[0]


def flat(blocks, keys):
    spots = [(j, at, x.shape[0]) for j, m in enumerate(keys) for at, x in blocks[m]]
    return spots, [x for m in keys for _, x in blocks[m]]


def add_rows(total, at, rows, values):
    done = []
    for start, old in total:
        size = old.shape[0]
        if at <= start and start + size <= at + rows:
            done.append((start, old + values[start - at : start - at + size]))
        elif start <= at and at + rows <= start + size:
            cuts = [(start, old[: at - start]), (at, old[at - start : at - start + rows] + values)]
            cuts.append((at + rows, old[at - start + rows :]))
            done += [c for c in cuts if c[1].shape[0]]
        else:
            done.append((start, old))
    return done


def product(spots, ins, tiles, side):
    total = None
    for (j, at, rows), x in zip(spots, ins):
        term = dot(x[...], tiles[j][...], 1, side)
        total = [(at, term)] if total is None else add_rows(total, at, rows, term)
    return total


def project_in(order, expert, blocks, keys, w_in, router):
    spots, xs = flat(blocks, keys)
    cap, width = 2 * blocks[0][0][1].shape[0], blocks[0][0][1].shape[1]
    hidden = w_in.shape[1]
    experts = router.shape[0]

    def kernel(order_ref, expert_ref, *refs):
        ins, (tiles, r_ref, a_ref, gate_ref) = refs[: len(xs)], refs[len(xs) :]
        scores = {}
        for (j, at, rows), x in zip(spots, ins):
            s = dot(x[...], r_ref[:, block_at(order_ref[j], width)], 1, 1)
            scores[at] = scores[at] + s if at in scores else s
            a = dot(x[...], tiles[j][...], 1, 0)
            if j == 0:
                a_ref[at : at + rows, :] = a
            else:
                a_ref[at : at + rows, :] += a
        for at, s in scores.items():
            mine = lax.broadcasted_iota(jnp.int32, s.shape, 1) == expert_ref[0]
            picked = jnp.sum(jnp.where(mine, s, 0.0), axis=1, keepdims=True)
            gate_ref[at : at + s.shape[0], :] = jax.nn.sigmoid(picked)

    flops = 2 * cap * width * len(keys) * hidden
    outs = [shaped(cap, hidden), shaped(cap, 1)]
    tiles = Tiles(w_in, 0, len(keys), hbm=True)
    return call(kernel, "project_in", flops, outs, [order, expert], *[[x] for x in xs], tiles, router)


def project_out(order, blocks, keys, w_out):
    spots, ys = flat(blocks, keys)
    cap, width = 2 * blocks[0][0][1].shape[0], blocks[0][0][1].shape[1]
    hidden = w_out.shape[0]

    def kernel(order_ref, *refs):
        ins, (w_ref, up) = refs[: len(ys)], refs[len(ys) :]
        for (j, at, rows), y in zip(spots, ins):
            u = dot(y[...], w_ref[:, block_at(order_ref[j], width)], 1, 1)
            if j == 0:
                up[at : at + rows, :] = u
            else:
                up[at : at + rows, :] += u

    flops = 2 * cap * width * len(keys) * hidden
    return call(kernel, "project_out", flops, [shaped(cap, hidden)], [order], *[[y] for y in ys], [w_out])[0]


def activation(order, blocks, keys, far, near, tiles, w_in, router_row, upstream, pre_act, gate):
    spots, ys = flat(blocks, keys)
    width = blocks[0][0][1].shape[1]
    cap, hidden = pre_act.shape
    count = sum(far) + sum(near)

    def kernel(order_ref, *refs):
        ins, refs = refs[: len(ys)], refs[len(ys) :]
        late, refs = refs[: len(tiles)], refs[len(tiles) :]
        back, r_ref, u_ref, a_ref, gate_ref, hg_ref, da_ref, ds_ref, *outs = refs
        up = [(0, u_ref[...])]
        for (j, at, rows), y in zip(spots, ins):
            up = add_rows(up, at, rows, dot(y[...], late[j][...], 1, 1))
        for at, u in up:
            place = slice(at, at + u.shape[0])
            a = a_ref[place, :]
            gate = gate_ref[place, :]
            sig = jax.nn.sigmoid(a)
            act = a * sig
            hg_ref[place, :] = (gate * act).astype(BF)
            gate_grad = jnp.sum(act * u, axis=1, keepdims=True)
            ds_ref[place, :] = gate_grad * gate * (1.0 - gate)
            da_ref[place, :] = (gate * u * sig * (1.0 + a * (1.0 - sig))).astype(BF)
        places = [(out, k) for out, n in zip(outs, far + near) for k in range(n)]
        for k, (out, spot) in enumerate(places):
            here = block_at(order_ref[k], width)
            block = dot(da_ref[...], back[k][...], 1, 1) + ds_ref[...] * r_ref[:, here]
            out[spot] = block.astype(out.dtype)

    flops = 2 * cap * width * (len(keys) + count) * hidden
    outs = [shaped(cap, hidden, dtype=BF), shaped(cap, hidden, dtype=BF), shaped(cap, 1)]
    outs += [shaped(n, cap, width, dtype=BF) for n in far] + [shaped(n, cap, width) for n in near]
    more = (Tiles(w_in, 0, count), router_row, upstream, pre_act, gate)
    return call(kernel, "activation", flops, outs, [order], *ys, *tiles, *more)


def router_column(order, blocks, keys, score_grad):
    spots, xs = flat(blocks, keys)
    width = blocks[0][0][1].shape[1]

    def kernel(order_ref, *refs):
        ins, (ds_ref, col) = refs[: len(xs)], refs[len(xs) :]
        for j in range(len(keys)):
            line = None
            for (k, at, rows), x in zip(spots, ins):
                if k == j:
                    c = jnp.sum(x[...].astype(F32) * ds_ref[at : at + rows, :], axis=0, keepdims=True)
                    line = c if line is None else line + c
            col[:, block_at(order_ref[j], width)] = line

    flops = 2 * score_grad.shape[0] * width * len(keys)
    outs = [shaped(1, width * len(keys))]
    return call(kernel, "router_column", flops, outs, [order], *[[x] for x in xs], score_grad)[0]


def grads_in(order, blocks, keys, pre_grad):
    spots, xs = flat(blocks, keys)
    cap, width = 2 * blocks[0][0][1].shape[0], blocks[0][0][1].shape[1]
    hidden = pre_grad.shape[1]

    def kernel(order_ref, *refs):
        ins, (da_ref, out) = refs[: len(xs)], refs[len(xs) :]
        for j in range(len(keys)):
            grad = None
            for (k, at, rows), x in zip(spots, ins):
                if k == j:
                    g = dot(x[...], da_ref[at : at + rows, :], 0, 0)
                    grad = g if grad is None else grad + g
            out[block_at(order_ref[j], width), :] = grad.astype(BF)

    flops = 2 * cap * width * len(keys) * hidden
    outs = [shaped(width * len(keys), hidden, dtype=BF)]
    return call(kernel, "grads_in", flops, outs, [order], *[[x] for x in xs], pre_grad)[0]


def grads_out(order, blocks, keys, gated):
    spots, ys = flat(blocks, keys)
    cap, width = 2 * blocks[0][0][1].shape[0], blocks[0][0][1].shape[1]
    hidden = gated.shape[1]

    def kernel(order_ref, *refs):
        ins, (hg_ref, out) = refs[: len(ys)], refs[len(ys) :]
        for j in range(len(keys)):
            grad = None
            for (k, at, rows), y in zip(spots, ins):
                if k == j:
                    g = dot(hg_ref[at : at + rows, :], y[...], 0, 0)
                    grad = g if grad is None else grad + g
            out[:, block_at(order_ref[j], width)] = grad.astype(BF)

    flops = 2 * cap * width * len(keys) * hidden
    outs = [shaped(hidden, width * len(keys), dtype=BF)]
    return call(kernel, "grads_out", flops, outs, [order], *[[y] for y in ys], gated)[0]


def numbers(values):
    return jnp.stack(values).astype(jnp.int32)


def body(tokens, cotangent, w_in, w_out, router, chosen):
    planes = lax.axis_size("plane")
    slots = 2 * lax.axis_size("tensor")
    tok_dev, features = tokens.shape
    width = features // slots
    cap = chosen.shape[1]
    plane = lax.axis_index("plane")
    half = lax.axis_index("half")
    slot = lax.axis_index("tensor") * 2 + half
    homes = 2 * planes
    bucket = 4 * tok_dev // homes
    expert = plane.astype(jnp.int32)[None]
    router_row = lax.dynamic_slice_in_dim(router.T, plane, 1, 0).astype(F32)
    masks = chip_masks(slots)
    firsts = numbers([(plane * 2 + half) * tok_dev] * 2)
    plane_firsts = numbers([(plane * 2 + part) * tok_dev for part in (0, half, 1 - half)])
    mine = lax.dynamic_slice_in_dim(chosen, plane, 1, 0)
    edges = jnp.arange(homes, dtype=jnp.int32)[:, None] * tok_dev
    reach = jnp.sum((mine < edges).astype(jnp.int32), axis=1)

    def columns(source, start, count):
        return lax.dynamic_slice_in_dim(source, start * width, count * width, 1)

    def exchange(x, axes):
        return lax.all_to_all(x, axes, split_axis=0, concat_axis=0, tiled=True)

    def order_of(*keys):
        return numbers([slot ^ m for m in keys])

    late = [m for m in masks if m.bit_count() > 1]
    early = [m for m in masks if m not in late]
    late_keys = late + [m | CORE for m in late]
    early_keys = early + [m | CORE for m in early]
    keys = early_keys + late_keys
    order = order_of(*keys)

    x_sent, hots = pack(firsts, chosen, [columns(tokens, slot // 2 * 2, 2)], bucket, True)
    x_got = exchange(x_sent, ("plane", "half"))
    cotangent, w_out, _ = join(cotangent, w_out, x_sent)
    y_own, y_away = columns(cotangent, slot, 1), flip(columns(cotangent, slot ^ 1, 1), 1)
    y_sent, _ = pack(plane_firsts, chosen, [y_own, y_away], 2 * bucket, False)
    tiles = [columns(w_out, slot ^ m, 1) for m in late_keys]
    x_got, y_sent, *tiles = join(x_got, y_sent, *tiles)

    y_got = exchange(y_sent, "plane")
    xs = plane_gather(*compact(reach, x_got, cap), slots)
    ready = [m for m in early if m]
    pieces = [x for m in ready for _, x in xs[m]]
    y_got, *pieces = join(y_got, *pieces)
    xs.update({m: [(at, pieces.pop(0)) for at, _ in xs[m]] for m in ready})
    add_core(xs, masks)

    pre_act, gate = project_in(order, expert, xs, keys, w_in, router.T)
    ys = plane_gather(*compact(reach[::2], y_got, cap), slots)
    tied = {m: [(at, after(x, pre_act)) for at, x in ys[m]] for m in early}
    add_core(tied, early)
    ys.update({m: tied[m] for m in tied if m & CORE})
    upstream = project_out(order_of(*early_keys), ys, early_keys, w_out)
    for m in late:
        ys[m] = [(at, after(x, upstream)) for at, x in ys[m]]
    add_core(ys, late)

    groups = [late[::-1], early[::-1]]
    sizes = [len(g) for g in groups]
    near = [m for g in groups for m in g]
    gated, pre_grad, score_grad, far1, far2, near1, near2 = activation(
        order_of(*[m | CORE for m in near], *near),
        ys,
        late_keys,
        sizes,
        sizes,
        tiles,
        w_in,
        router_row,
        upstream,
        pre_act,
        gate,
    )
    hops = [
        lambda x, step=1 << i: lax.ppermute(x, "plane", [(e, e ^ step) for e in range(planes)])
        for i in range(planes.bit_length() - 1)
    ]
    hops += [functools.partial(flip, bit=1 << i) for i in reversed(range(slots.bit_length() - 1))]

    def hop(total):
        return total + hops.pop(0)(total) if hops else total

    mid = cap // 2
    got1 = flip(far1, CORE)
    got1, near1, score_grad, far2 = join(got1, near1, score_grad, far2)
    got2 = flip(far2, CORE)
    sums = {m: near1[k] + got1[k].astype(F32) for k, m in enumerate(groups[0])}
    column = router_column(order, xs, keys, score_grad)
    sums.update({m: near2[k] + got2[k].astype(F32) for k, m in enumerate(groups[1])})
    for m in groups[0]:
        low, high = m & -m, top_bit(m)
        a, b = flip(sums[m][:mid].astype(BF), low), flip(sums[m][mid:].astype(BF), high)
        a, b, column, *rest = join(a, b, column, *[sums[k] for k in groups[1]])
        sums.update(zip(groups[1], rest))
        pad = jnp.zeros((cap - mid, width), F32)
        sums[m ^ low] = sums[m ^ low] + jnp.concatenate([a.astype(F32), pad])
        sums[m ^ high] = sums[m ^ high] + jnp.concatenate([pad, b.astype(F32)])
    sent = [sums[m].astype(BF) for m in groups[1] if m]
    *sent, column, pre_grad = join(*sent, column, pre_grad)
    came = [flip(x, m) for x, m in zip(sent, groups[1])]
    total = jnp.where(jnp.arange(planes)[:, None] == plane, column, 0.0)
    total = hop(total)
    grad_in = grads_in(order, xs, keys, pre_grad)
    total = hop(total)
    *terms, grad_in, total = join(sums[0], *came, grad_in, total)

    back = place(reach, homes, bucket, terms)
    returned = exchange(back, ("plane", "half"))
    grad_out = grads_out(order, ys, keys, after(gated, back))
    total = after(total, grad_out)
    while hops:
        total = hop(total)
    returned, grad_out, total = join(returned, grad_out, total)
    return (combine(hots, returned), grad_in, grad_out, total.T)


def solution(mesh):
    planes = mesh.shape["expert"] // 2
    inner = Mesh(mesh.devices.reshape(planes, 2, mesh.shape["tensor"]), ("plane", "half", "tensor"))
    home = ("plane", "half")
    every = ("plane", "half", "tensor")
    return jax.shard_map(
        body,
        mesh=inner,
        in_specs=(P(home, None), P(home, None), P(None, every), P(every, None), P(), P()),
        out_specs=(P(home, "tensor"), P(None, every), P(every, None), P()),
        check_vma=False,
    )
```

```python
import functools
import math

import jax
import jax.numpy as jnp
from jax import lax
from jax.experimental import pallas as pl
from jax.experimental.pallas import tpu as pltpu
from jax.sharding import Mesh
from jax.sharding import PartitionSpec as P

BF = jnp.bfloat16
F32 = jnp.float32
CORE = 2
VMEM_LIMIT = 24 * 1024 * 1024


def dot(a, b, da, db):
    return lax.dot_general(a, b, (((da,), (db,)), ((), ())), preferred_element_type=F32)


def flip(x, bit):
    if bit == 1:
        return lax.ppermute(x, "half", [(0, 1), (1, 0)])
    n = lax.axis_size("tensor")
    return lax.ppermute(x, "tensor", [(i, i ^ (bit >> 1)) for i in range(n)])


def chip_masks(slots):
    return sorted((m for m in range(slots) if not m & CORE), key=lambda m: (m.bit_count(), m))


def top_bit(m):
    return 1 << (m.bit_length() - 1)


def plane_gather(top, bottom, slots):
    half = top.shape[0]
    blocks = {0: [(0, top), (half, bottom)]}
    for m in chip_masks(slots)[1:]:
        low, high = m & -m, top_bit(m)
        first, second = (blocks[0], blocks[0]) if low == high else (blocks[m ^ low], blocks[m ^ high])
        blocks[m] = [(0, flip(first[0][1], low)), (half, flip(second[1][1], high))]
    return blocks


def add_core(blocks, masks):
    for m in masks:
        blocks[m | CORE] = [(at, flip(x, CORE)) for at, x in blocks[m]]


def after(x, *others):
    return lax.optimization_barrier((x, *others))[0]


def join(*arrays):
    return lax.optimization_barrier(arrays)


def in_hbm(x):
    return pltpu.with_memory_space_constraint(x, pltpu.HBM)


class Tiles:
    def __init__(self, x, axis, count, hbm=False):
        self.x, self.axis, self.count = x, axis, count
        if hbm:
            self.x = in_hbm(x)
        self.size = x.shape[axis] // (2 * lax.axis_size("tensor"))

    def at(self, ref, order_ref, j):
        here = block_at(order_ref[j], self.size)
        return ref.at[here, :] if self.axis == 0 else ref.at[:, here]


def call(kernel, name, flops, outs, smem, *args):
    flat_args = list(smem)
    for x in args:
        if isinstance(x, Tiles):
            x = x.x
        elif isinstance(x, list):
            x = in_hbm(x[0])
        flat_args.append(x)

    def run(*refs):
        scalars, refs = refs[: len(smem)], list(refs[len(smem) :])
        for i, x in enumerate(args):
            if isinstance(x, Tiles):
                refs[i] = [x.at(refs[i], scalars[0], j) for j in range(x.count)]
        kernel(*scalars, *refs)

    moved = sum(a.size * a.dtype.itemsize for a in flat_args) + 4 * sum(math.prod(o.shape) for o in outs)
    return pl.pallas_call(
        run,
        in_specs=[pl.BlockSpec(memory_space=pltpu.SMEM)] * len(smem)
        + [pl.BlockSpec(memory_space=pltpu.VMEM)] * len(args),
        out_specs=[pl.BlockSpec(memory_space=pltpu.VMEM)] * len(outs),
        out_shape=outs,
        compiler_params=pltpu.CompilerParams(vmem_limit_bytes=VMEM_LIMIT),
        cost_estimate=pl.CostEstimate(flops=int(flops), bytes_accessed=int(moved), transcendentals=0),
        name=name,
    )(*flat_args)


def shaped(*shape, dtype=F32):
    return jax.ShapeDtypeStruct(shape, dtype)


def block_at(start, size):
    return pl.ds(pl.multiple_of(start * size, size), size)


def pack(firsts, chosen, sources, bucket, halves):
    experts, cap = chosen.shape
    rows, width = sources[0].shape

    def kernel(firsts_ref, chosen_ref, *refs):
        ins, (out, hot_out) = refs[: len(sources)], refs[len(sources) :]
        for e in range(experts):
            line = chosen_ref[e : e + 1, :]
            start = jnp.sum((line < firsts_ref[0]).astype(jnp.int32))
            line = pltpu.roll(jnp.broadcast_to(line, (8, cap)), cap - start, 1)[:1, :bucket]
            got = None
            for i, x in enumerate(ins):
                hot = lax.broadcasted_iota(jnp.int32, (rows, bucket), 0) == line - firsts_ref[i + 1]
                hot = hot.astype(F32).astype(BF)
                hot_out[e] = hot
                term = dot(hot, x[...], 0, 0)
                got = term if got is None else got + term
            got = got.astype(BF)
            if halves:
                out[2 * e], out[2 * e + 1] = got[:, : width // 2], got[:, width // 2 :]
            else:
                out[e] = got

    flops = 2 * experts * bucket * rows * width * len(sources)
    parts = 2 if halves else 1
    outs = [
        pltpu.HBM((experts * parts, bucket, width // parts), BF),
        pltpu.HBM((experts, rows, bucket), BF),
    ]
    return call(kernel, "pack_rows", flops, outs, [firsts], chosen, *sources)


def compact(reach, buckets, cap):
    homes, bucket, width = buckets.shape

    def kernel(reach_ref, buckets_ref, top, bottom):
        acc = None
        for s in range(homes):
            at = lax.broadcasted_iota(jnp.int32, (cap, bucket), 0) - reach_ref[s]
            hot = lax.broadcasted_iota(jnp.int32, (cap, bucket), 1) == at
            term = dot(hot.astype(F32).astype(BF), buckets_ref[s], 1, 0)
            acc = term if acc is None else acc + term
        top[...], bottom[...] = acc[: cap // 2].astype(BF), acc[cap // 2 :].astype(BF)

    flops = 2 * cap * homes * bucket * width
    outs = [shaped(cap // 2, width, dtype=BF)] * 2
    return call(kernel, "compact_rows", flops, outs, [reach], buckets)


def place(reach, homes, bucket, terms):
    cap, width = terms[0].shape

    def kernel(reach_ref, *refs):
        total = refs[0][...].astype(F32)
        for r in refs[1:-1]:
            total = total + r[...].astype(F32)
        rows = total.astype(BF)
        for s in range(homes):
            at = lax.broadcasted_iota(jnp.int32, (bucket, cap), 1) - reach_ref[s]
            hot = lax.broadcasted_iota(jnp.int32, (bucket, cap), 0) == at
            refs[-1][s] = dot(hot.astype(F32).astype(BF), rows, 1, 0).astype(BF)

    flops = 2 * cap * homes * bucket * width
    outs = [pltpu.HBM((homes, bucket, width), BF)]
    return call(kernel, "place_rows", flops, outs, [reach], *terms)[0]


def combine(hots, returned):
    experts, rows, bucket = hots.shape
    width = returned.shape[2]

    def kernel(hots_ref, returned_ref, out):
        for h in range(2):
            acc = None
            for e in range(experts):
                term = dot(hots_ref[e], returned_ref[2 * e + h], 1, 0)
                acc = term if acc is None else acc + term
            out[:, h * width : (h + 1) * width] = acc.astype(BF)

    flops = 4 * experts * bucket * rows * width
    outs = [shaped(rows, 2 * width, dtype=BF)]
    return call(kernel, "combine_rows", flops, outs, [], hots, returned)[0]


def flat(blocks, keys):
    spots = [(j, at, x.shape[0]) for j, m in enumerate(keys) for at, x in blocks[m]]
    return spots, [x for m in keys for _, x in blocks[m]]


def add_rows(total, at, rows, values):
    done = []
    for start, old in total:
        size = old.shape[0]
        if at <= start and start + size <= at + rows:
            done.append((start, old + values[start - at : start - at + size]))
        elif start <= at and at + rows <= start + size:
            cuts = [(start, old[: at - start]), (at, old[at - start : at - start + rows] + values)]
            cuts.append((at + rows, old[at - start + rows :]))
            done += [c for c in cuts if c[1].shape[0]]
        else:
            done.append((start, old))
    return done


def product(spots, ins, tiles, side):
    total = None
    for (j, at, rows), x in zip(spots, ins):
        term = dot(x[...], tiles[j][...], 1, side)
        total = [(at, term)] if total is None else add_rows(total, at, rows, term)
    return total


def project_in(order, expert, blocks, keys, w_in, router):
    spots, xs = flat(blocks, keys)
    cap, width = 2 * blocks[0][0][1].shape[0], blocks[0][0][1].shape[1]
    hidden = w_in.shape[1]
    experts = router.shape[0]

    def kernel(order_ref, expert_ref, *refs):
        ins, (tiles, r_ref, a_ref, gate_ref) = refs[: len(xs)], refs[len(xs) :]
        scores = {}
        for (j, at, rows), x in zip(spots, ins):
            s = dot(x[...], r_ref[:, block_at(order_ref[j], width)], 1, 1)
            scores[at] = scores[at] + s if at in scores else s
            a = dot(x[...], tiles[j][...], 1, 0)
            if j == 0:
                a_ref[at : at + rows, :] = a
            else:
                a_ref[at : at + rows, :] += a
        for at, s in scores.items():
            mine = lax.broadcasted_iota(jnp.int32, s.shape, 1) == expert_ref[0]
            picked = jnp.sum(jnp.where(mine, s, 0.0), axis=1, keepdims=True)
            gate_ref[at : at + s.shape[0], :] = jax.nn.sigmoid(picked)

    flops = 2 * cap * width * len(keys) * hidden
    outs = [shaped(cap, hidden), shaped(cap, 1)]
    tiles = Tiles(w_in, 0, len(keys), hbm=True)
    return call(kernel, "project_in", flops, outs, [order, expert], *[[x] for x in xs], tiles, router)


def project_out(order, blocks, keys, w_out):
    spots, ys = flat(blocks, keys)
    cap, width = 2 * blocks[0][0][1].shape[0], blocks[0][0][1].shape[1]
    hidden = w_out.shape[0]

    def kernel(order_ref, *refs):
        ins, (w_ref, up) = refs[: len(ys)], refs[len(ys) :]
        for (j, at, rows), y in zip(spots, ins):
            u = dot(y[...], w_ref[:, block_at(order_ref[j], width)], 1, 1)
            if j == 0:
                up[at : at + rows, :] = u
            else:
                up[at : at + rows, :] += u

    flops = 2 * cap * width * len(keys) * hidden
    return call(kernel, "project_out", flops, [shaped(cap, hidden)], [order], *[[y] for y in ys], [w_out])[0]


def activation(order, blocks, keys, far, near, tiles, w_in, router_row, upstream, pre_act, gate):
    spots, ys = flat(blocks, keys)
    width = blocks[0][0][1].shape[1]
    cap, hidden = pre_act.shape
    count = sum(far) + sum(near)

    def kernel(order_ref, *refs):
        ins, refs = refs[: len(ys)], refs[len(ys) :]
        late, refs = refs[: len(tiles)], refs[len(tiles) :]
        back, r_ref, u_ref, a_ref, gate_ref, hg_ref, da_ref, ds_ref, *outs = refs
        up = [(0, u_ref[...])]
        for (j, at, rows), y in zip(spots, ins):
            up = add_rows(up, at, rows, dot(y[...], late[j][...], 1, 1))
        for at, u in up:
            place = slice(at, at + u.shape[0])
            a = a_ref[place, :]
            gate = gate_ref[place, :]
            sig = jax.nn.sigmoid(a)
            act = a * sig
            hg_ref[place, :] = (gate * act).astype(BF)
            gate_grad = jnp.sum(act * u, axis=1, keepdims=True)
            ds_ref[place, :] = gate_grad * gate * (1.0 - gate)
            da_ref[place, :] = (gate * u * sig * (1.0 + a * (1.0 - sig))).astype(BF)
        places = [(out, k) for out, n in zip(outs, far + near) for k in range(n)]
        for k, (out, spot) in enumerate(places):
            here = block_at(order_ref[k], width)
            block = dot(da_ref[...], back[k][...], 1, 1) + ds_ref[...] * r_ref[:, here]
            out[spot] = block.astype(out.dtype)

    flops = 2 * cap * width * (len(keys) + count) * hidden
    outs = [shaped(cap, hidden, dtype=BF), shaped(cap, hidden, dtype=BF), shaped(cap, 1)]
    outs += [shaped(n, cap, width, dtype=BF) for n in far] + [shaped(n, cap, width) for n in near]
    more = (Tiles(w_in, 0, count), router_row, upstream, pre_act, gate)
    return call(kernel, "activation", flops, outs, [order], *ys, *tiles, *more)


def router_column(order, blocks, keys, score_grad):
    spots, xs = flat(blocks, keys)
    width = blocks[0][0][1].shape[1]

    def kernel(order_ref, *refs):
        ins, (ds_ref, col) = refs[: len(xs)], refs[len(xs) :]
        for j in range(len(keys)):
            line = None
            for (k, at, rows), x in zip(spots, ins):
                if k == j:
                    c = jnp.sum(x[...].astype(F32) * ds_ref[at : at + rows, :], axis=0, keepdims=True)
                    line = c if line is None else line + c
            col[:, block_at(order_ref[j], width)] = line

    flops = 2 * score_grad.shape[0] * width * len(keys)
    outs = [shaped(1, width * len(keys))]
    return call(kernel, "router_column", flops, outs, [order], *[[x] for x in xs], score_grad)[0]


def grads_in(order, blocks, keys, pre_grad):
    spots, xs = flat(blocks, keys)
    cap, width = 2 * blocks[0][0][1].shape[0], blocks[0][0][1].shape[1]
    hidden = pre_grad.shape[1]

    def kernel(order_ref, *refs):
        ins, (da_ref, out) = refs[: len(xs)], refs[len(xs) :]
        for j in range(len(keys)):
            grad = None
            for (k, at, rows), x in zip(spots, ins):
                if k == j:
                    g = dot(x[...], da_ref[at : at + rows, :], 0, 0)
                    grad = g if grad is None else grad + g
            out[block_at(order_ref[j], width), :] = grad.astype(BF)

    flops = 2 * cap * width * len(keys) * hidden
    outs = [shaped(width * len(keys), hidden, dtype=BF)]
    return call(kernel, "grads_in", flops, outs, [order], *[[x] for x in xs], pre_grad)[0]


def grads_out(order, blocks, keys, gated):
    spots, ys = flat(blocks, keys)
    cap, width = 2 * blocks[0][0][1].shape[0], blocks[0][0][1].shape[1]
    hidden = gated.shape[1]

    def kernel(order_ref, *refs):
        ins, (hg_ref, out) = refs[: len(ys)], refs[len(ys) :]
        for j in range(len(keys)):
            grad = None
            for (k, at, rows), y in zip(spots, ins):
                if k == j:
                    g = dot(hg_ref[at : at + rows, :], y[...], 0, 0)
                    grad = g if grad is None else grad + g
            out[:, block_at(order_ref[j], width)] = grad.astype(BF)

    flops = 2 * cap * width * len(keys) * hidden
    outs = [shaped(hidden, width * len(keys), dtype=BF)]
    return call(kernel, "grads_out", flops, outs, [order], *[[y] for y in ys], gated)[0]


def numbers(values):
    return jnp.stack(values).astype(jnp.int32)


def body(tokens, cotangent, w_in, w_out, router, chosen):
    planes = lax.axis_size("plane")
    slots = 2 * lax.axis_size("tensor")
    tok_dev, features = tokens.shape
    width = features // slots
    cap = chosen.shape[1]
    plane = lax.axis_index("plane")
    half = lax.axis_index("half")
    slot = lax.axis_index("tensor") * 2 + half
    homes = 2 * planes
    bucket = 4 * tok_dev // homes
    expert = plane.astype(jnp.int32)[None]
    router_row = lax.dynamic_slice_in_dim(router.T, plane, 1, 0).astype(F32)
    masks = chip_masks(slots)
    firsts = numbers([(plane * 2 + half) * tok_dev] * 2)
    plane_firsts = numbers([(plane * 2 + part) * tok_dev for part in (0, half, 1 - half)])
    mine = lax.dynamic_slice_in_dim(chosen, plane, 1, 0)
    edges = jnp.arange(homes, dtype=jnp.int32)[:, None] * tok_dev
    reach = jnp.sum((mine < edges).astype(jnp.int32), axis=1)

    def columns(source, start, count):
        return lax.dynamic_slice_in_dim(source, start * width, count * width, 1)

    def exchange(x, axes):
        return lax.all_to_all(x, axes, split_axis=0, concat_axis=0, tiled=True)

    def order_of(*keys):
        return numbers([slot ^ m for m in keys])

    late = [m for m in masks if m.bit_count() > 1]
    early = [m for m in masks if m not in late]
    late_keys = late + [m | CORE for m in late]
    early_keys = early + [m | CORE for m in early]
    keys = early_keys + late_keys
    order = order_of(*keys)

    x_sent, hots = pack(firsts, chosen, [columns(tokens, slot // 2 * 2, 2)], bucket, True)
    x_got = exchange(x_sent, ("plane", "half"))
    cotangent, w_out, _ = join(cotangent, w_out, x_sent)
    y_own, y_away = columns(cotangent, slot, 1), flip(columns(cotangent, slot ^ 1, 1), 1)
    y_sent, _ = pack(plane_firsts, chosen, [y_own, y_away], 2 * bucket, False)
    tiles = [columns(w_out, slot ^ m, 1) for m in late_keys]
    x_got, y_sent, *tiles = join(x_got, y_sent, *tiles)

    y_got = exchange(y_sent, "plane")
    xs = plane_gather(*compact(reach, x_got, cap), slots)
    ready = [m for m in early if m]
    pieces = [x for m in ready for _, x in xs[m]]
    y_got, *pieces = join(y_got, *pieces)
    xs.update({m: [(at, pieces.pop(0)) for at, _ in xs[m]] for m in ready})
    add_core(xs, masks)

    pre_act, gate = project_in(order, expert, xs, keys, w_in, router.T)
    ys = plane_gather(*compact(reach[::2], y_got, cap), slots)
    tied = {m: [(at, after(x, pre_act)) if m else (at, x) for at, x in ys[m]] for m in early}
    add_core(tied, early)
    ys.update({m: tied[m] for m in tied if m & CORE})
    upstream = project_out(order_of(*early_keys), ys, early_keys, w_out)
    for m in late:
        ys[m] = [(at, after(x, upstream)) for at, x in ys[m]]
    add_core(ys, late)

    groups = [late[::-1], early[::-1]]
    sizes = [len(g) for g in groups]
    near = [m for g in groups for m in g]
    gated, pre_grad, score_grad, far1, far2, near1, near2 = activation(
        order_of(*[m | CORE for m in near], *near),
        ys,
        late_keys,
        sizes,
        sizes,
        tiles,
        w_in,
        router_row,
        upstream,
        pre_act,
        gate,
    )
    hops = [
        lambda x, step=1 << i: lax.ppermute(x, "plane", [(e, e ^ step) for e in range(planes)])
        for i in range(planes.bit_length() - 1)
    ]
    hops += [functools.partial(flip, bit=1 << i) for i in reversed(range(slots.bit_length() - 1))]

    def hop(total):
        return total + hops.pop(0)(total) if hops else total

    mid = cap // 2
    got1 = flip(far1, CORE)
    got1, near1, score_grad, far2 = join(got1, near1, score_grad, far2)
    got2 = flip(far2, CORE)
    sums = {m: near1[k] + got1[k].astype(F32) for k, m in enumerate(groups[0])}
    column = router_column(order, xs, keys, score_grad)
    sums.update({m: near2[k] + got2[k].astype(F32) for k, m in enumerate(groups[1])})
    for m in groups[0]:
        low, high = m & -m, top_bit(m)
        a, b = flip(sums[m][:mid].astype(BF), low), flip(sums[m][mid:].astype(BF), high)
        a, b, column, *rest = join(a, b, column, *[sums[k] for k in groups[1]])
        sums.update(zip(groups[1], rest))
        pad = jnp.zeros((cap - mid, width), F32)
        sums[m ^ low] = sums[m ^ low] + jnp.concatenate([a.astype(F32), pad])
        sums[m ^ high] = sums[m ^ high] + jnp.concatenate([pad, b.astype(F32)])
    sent = [sums[m].astype(BF) for m in groups[1] if m]
    *sent, pre_grad = join(*sent, pre_grad)
    came = [flip(x, m) for x, m in zip(sent, groups[1])]
    total = jnp.where(jnp.arange(planes)[:, None] == plane, column, 0.0)
    total = hop(total)
    grad_in = grads_in(order, xs, keys, pre_grad)
    total = hop(total)
    *terms, grad_in, total = join(sums[0], *came, grad_in, total)

    back = place(reach, homes, bucket, terms)
    returned = exchange(back, ("plane", "half"))
    grad_out = grads_out(order, ys, keys, after(gated, back))
    total = after(total, grad_out)
    while hops:
        total = hop(total)
    returned, grad_out, total = join(returned, grad_out, total)
    return (combine(hots, returned), grad_in, grad_out, total.T)


def solution(mesh):
    planes = mesh.shape["expert"] // 2
    inner = Mesh(mesh.devices.reshape(planes, 2, mesh.shape["tensor"]), ("plane", "half", "tensor"))
    home = ("plane", "half")
    every = ("plane", "half", "tensor")
    return jax.shard_map(
        body,
        mesh=inner,
        in_specs=(P(home, None), P(home, None), P(None, every), P(every, None), P(), P()),
        out_specs=(P(home, "tensor"), P(None, every), P(every, None), P()),
        check_vma=False,
    )
```
